256 devices in a mesh: tok: 64 (over y, z, core), head: 4 (over x).
Axes of the slice: x: 4, y: 4, z: 8, core: 2. Of those that a mesh axis runs over, the one named last changes fastest.
Arguments:
- keys: bfloat16 [32768, 3072], P('tok', 'head'), may hold values from -6 to 6
- values: bfloat16 [32768, 3072], P('tok', 'head'), may hold values from -6 to 6
- rates: float32 [32768, 4], P('tok', 'head'), may hold values from 0.01 to 1
- fast_weights: bfloat16 [4, 3, 768, 768], P('head'), may hold values from -0.109375 to 0.109375
- queries: bfloat16 [16384, 3072], P('tok', 'head'), may hold values from -6 to 6
- out_proj: bfloat16 [3072, 3072], P('head'), may hold values from -0.109375 to 0.109375
Outputs:
- mixed: bfloat16 [3072, 16384], P('head', 'tok')
The draws below stay inside these ranges and needn't reach their ends.
All inputs are finite; a program needn't handle non-finite values.
Results may differ from the reference program's by a relative error of at most 0.015.
Values may be sent and summed in bfloat16 or wider, within the bound.
No kernel may reach another device: no remote copies, remote signals or barrier semaphores. Data moves between devices by JAX's collectives and lax.ppermute only.
A program may use at most 128 MiB of HBM per device.

```python
import math
import jax
import jax.numpy as jnp
from jax import lax

DH = 768
NS_ITERS = 2
HEADS = 4
MODEL = 3072
TOKENS = 32768
TARGETS = 16384


def levels(own_key, dims, pieces, smallest, largest):
    loudness = 1.0
    for dim, shards_of in pieces:
        draws = jax.random.uniform(jax.random.fold_in(jax.random.fold_in(own_key, 6), dim), (shards_of,), jnp.float32, smallest / len(pieces), largest / len(pieces))
        loudness = loudness * jnp.repeat(jnp.exp(draws), dims[dim] // shards_of).reshape((-1,) + (1,) * (len(dims) - 1 - dim))
    return loudness


def scatter_about(stream_key, dims, scale, most, pieces=(), kind=jnp.bfloat16):
    drawn = jax.random.normal(stream_key, dims, jnp.float32) * scale
    if len(pieces) > 0:
        drawn = levels(stream_key, dims, pieces, -0.22, 0.18) * drawn
    return jnp.clip(drawn, min=-most, max=most).astype(kind)


def setup_inputs(seed: int = 0) -> dict:
    arg_keys = jax.random.split(jax.random.key(seed), 7)
    keys = scatter_about(arg_keys[0], (TOKENS, HEADS * DH), 1.0, 6.0, ((0, 64), (1, 4)))
    values = scatter_about(arg_keys[1], (TOKENS, HEADS * DH), 1.0, 6.0, ((0, 64), (1, 4)))
    rates = jnp.clip(jnp.exp(math.log(1.0) - 4.6051702 * jax.random.uniform(arg_keys[2], (TOKENS, HEADS), jnp.float32) ** levels(arg_keys[2], (TOKENS, HEADS), ((0, 64), (1, 4)), -0.2, 0.2)), 0.01, 1.0)
    fast_weights = scatter_about(arg_keys[3], (HEADS, 3, DH, DH), (4 * DH) ** -0.5, 0.109375, ((0, 4),))
    queries = scatter_about(arg_keys[4], (TARGETS, HEADS * DH), 1.0, 6.0, ((0, 64), (1, 4)))
    out_proj = scatter_about(arg_keys[5], (MODEL, MODEL), MODEL ** -0.5, 0.109375, ((0, 4),))
    return dict(keys=keys, values=values, rates=rates, fast_weights=fast_weights, queries=queries, out_proj=out_proj)


ns_a = 3.4445
ns_b = -4.775
ns_c = 2.0315
step_scale = 1.0
eps = 1e-07

def silu_slope(pre):
    sig = jax.nn.sigmoid(pre)
    return sig * (1.0 + pre * (1.0 - sig))

def head_grads(keys_h, values_h, rates_h, weights):
    h1 = jnp.dot(keys_h, weights[0], preferred_element_type=jnp.float32)
    h3 = jnp.dot(keys_h, weights[1], preferred_element_type=jnp.float32)
    act = jax.nn.silu(h1)
    hidden = (act * h3).astype(jnp.bfloat16)
    errors = (-rates_h[:, None] * values_h.astype(jnp.float32)).astype(jnp.bfloat16)
    grad_two = jnp.dot(hidden.T, errors, preferred_element_type=jnp.float32)
    dz = jnp.dot(errors, weights[2].T, preferred_element_type=jnp.float32)
    grad_pre1 = (dz * h3 * silu_slope(h1)).astype(jnp.bfloat16)
    grad_pre3 = (dz * act).astype(jnp.bfloat16)
    grad_one = jnp.dot(keys_h.T, grad_pre1, preferred_element_type=jnp.float32)
    grad_three = jnp.dot(keys_h.T, grad_pre3, preferred_element_type=jnp.float32)
    return jnp.stack([grad_one, grad_three, grad_two])

def orthogonal(grads):
    norms = jnp.sqrt(lax.optimization_barrier(jnp.sum(grads * grads, axis=(1, 2))))
    iterate = (grads / (norms[:, None, None] + eps)).astype(jnp.bfloat16)
    for turn in range(NS_ITERS):
        wide = iterate.astype(jnp.float32)
        gram = jnp.einsum('mij,mkj->mik', wide, wide).astype(jnp.bfloat16)
        gram_wide = gram.astype(jnp.float32)
        poly = (ns_b * gram_wide + ns_c * jnp.einsum('mij,mjk->mik', gram_wide, gram_wide)).astype(jnp.bfloat16)
        iterate = (ns_a * wide + jnp.einsum('mij,mjk->mik', poly.astype(jnp.float32), wide)).astype(jnp.bfloat16)
    return iterate

def reference(keys, values, rates, fast_weights, queries, out_proj):
    total = jnp.zeros((out_proj.shape[0], queries.shape[0]), jnp.float32)
    for head in range(HEADS):
        cols = slice(head * DH, (head + 1) * DH)
        weights = fast_weights[head]
        grads = head_grads(keys[:, cols], values[:, cols], rates[:, head], weights)
        update = orthogonal(grads)
        fresh = (weights.astype(jnp.float32) - step_scale * update.astype(jnp.float32)).astype(jnp.bfloat16)
        query_h = queries[:, cols]
        q1 = jnp.dot(query_h, fresh[0], preferred_element_type=jnp.float32)
        q3 = jnp.dot(query_h, fresh[1], preferred_element_type=jnp.float32)
        gated = (jax.nn.silu(q1) * q3).astype(jnp.bfloat16)
        outputs = jnp.dot(gated, fresh[2], preferred_element_type=jnp.float32).astype(jnp.bfloat16)
        total = total + jnp.dot(out_proj[cols, :].T, outputs.T, preferred_element_type=jnp.float32)
    return total.astype(jnp.bfloat16)
```

```python
import jax
import jax.numpy as jnp
from jax import lax
from jax.sharding import PartitionSpec as P

NS_ITERS = 2


ns_a = 3.4445
ns_b = -4.775
ns_c = 2.0315
step_scale = 1.0
eps = 1e-07

f32 = jnp.float32
bf16 = jnp.bfloat16

NY, NZ, NC = 4, 8, 2


def chip_index(y, z, core):
    return (y * NZ + z) * NC + core


Y_GROUPS = [
    [chip_index(y, z, core) for y in range(NY)] for z in range(NZ) for core in range(NC)
]
Z_GROUPS = [
    [chip_index(y, z, core) for z in range(NZ)] for y in range(NY) for core in range(NC)
]
CORE_SWAP = [(device, device ^ 1) for device in range(NY * NZ * NC)]


def silu_slope(pre):
    sig = jax.nn.sigmoid(pre)
    return sig * (1.0 + pre * (1.0 - sig))


def swap_cores(array):
    return lax.ppermute(array, "tok", CORE_SWAP)


def exchange(blocks, groups):
    return lax.all_to_all(blocks, "tok", 0, 0, axis_index_groups=groups)


def sum_shares(blocks, groups):
    return jnp.sum(exchange(blocks, groups).astype(f32), axis=0).astype(bf16)


def gather_rows(rows, groups):
    size = len(groups[0])
    gathered = exchange(jnp.broadcast_to(rows[None], (size,) + rows.shape), groups)
    return gathered.reshape(-1, rows.shape[1])


def outer(left, right):
    return lax.dot_general(left, right, (((1,), (1,)), ((), ())), preferred_element_type=f32)


def orthogonal(parts):
    square_sum = sum(jnp.sum(part.astype(f32) * part.astype(f32)) for part in parts)
    scale = 1.0 / (jnp.sqrt(square_sum) + eps)
    for turn in range(NS_ITERS):
        gram = sum(outer(part, part) for part in parts)
        if turn == 0:
            gram = gram * (scale * scale)
        gram = gram.astype(bf16)
        squared = jnp.dot(gram, gram, preferred_element_type=f32)
        poly = (ns_b * gram.astype(f32) + ns_c * squared).astype(bf16)
        new = []
        for part in parts:
            applied = jnp.dot(poly, part, preferred_element_type=f32)
            applied = ns_a * part.astype(f32) + applied
            if turn == 0:
                applied = applied * scale
            new.append(applied.astype(bf16))
        parts = new
    return parts


def on_device(keys, values, rates, fast_weights, queries, out_proj):
    weights = fast_weights[0]
    width = weights.shape[1]
    half = width // 2
    core = lax.axis_index("tok") % NC
    head = lax.axis_index("head")
    first = core == 0

    h1 = jnp.dot(keys, weights[0], preferred_element_type=f32)
    h3 = jnp.dot(keys, weights[1], preferred_element_type=f32)
    act = jax.nn.silu(h1)
    hidden = (act * h3).astype(bf16)
    errors = (-rates * values.astype(f32)).astype(bf16)

    def token_sum(left, right):
        return lax.dot_general(left, right, (((0,), (0,)), ((), ())), preferred_element_type=f32)

    errors_keep = lax.dynamic_slice_in_dim(errors, core * half, half, 1)
    errors_send = lax.dynamic_slice_in_dim(errors, (1 - core) * half, half, 1)
    shared_got = swap_cores(token_sum(hidden, errors_send).astype(bf16))
    shared_keep = token_sum(hidden, errors_keep)
    dz = outer(errors, weights[2])
    grad_pre1 = (dz * h3 * silu_slope(h1)).astype(bf16)
    grad_pre3 = (dz * act).astype(bf16)
    own_got = swap_cores(token_sum(keys, jnp.where(first, grad_pre3, grad_pre1)).astype(bf16))
    own_keep = token_sum(keys, jnp.where(first, grad_pre1, grad_pre3))
    chip_sum = jnp.concatenate(
        [own_keep + own_got.astype(f32), shared_keep + shared_got.astype(f32)], axis=1
    ).astype(bf16)

    y_sum = sum_shares(chip_sum.reshape(NY, width // NY, -1), Y_GROUPS)
    z_sum = sum_shares(y_sum.reshape(NZ, width // NY // NZ, -1), Z_GROUPS)
    summed = gather_rows(gather_rows(z_sum, Z_GROUPS), Y_GROUPS)

    shared_part = summed[:, width:]
    shared_other = swap_cores(shared_part)
    (own_update,) = orthogonal([summed[:, :width]])
    own_weights = jnp.where(first, weights[0], weights[1])
    own_fresh = (own_weights.astype(f32) - step_scale * own_update.astype(f32)).astype(bf16)
    other_fresh = swap_cores(own_fresh)
    left = jnp.where(first, shared_part, shared_other)
    right = jnp.where(first, shared_other, shared_part)
    (shared_update,) = orthogonal([jnp.concatenate([left, right], axis=1)])
    shared_fresh = (weights[2].astype(f32) - step_scale * shared_update.astype(f32)).astype(bf16)

    q_own = jnp.dot(queries, own_fresh, preferred_element_type=f32)
    q_other = jnp.dot(queries, other_fresh, preferred_element_type=f32)
    q1 = jnp.where(first, q_own, q_other)
    q3 = jnp.where(first, q_other, q_own)
    gated = (jax.nn.silu(q1) * q3).astype(bf16)
    outputs = jnp.dot(gated, shared_fresh, preferred_element_type=f32).astype(bf16)

    heads = lax.axis_size("head")

    def contribution(target):
        columns = lax.dynamic_slice_in_dim(out_proj, target * width, width, 1)
        return lax.dot_general(columns, outputs, (((0,), (1,)), ((), ())), preferred_element_type=f32)

    got = []
    for step in (2, 1, 3):
        part = contribution((head + step) % heads).astype(bf16)
        got.append(
            lax.ppermute(part, "head", [(i, (i + step) % heads) for i in range(heads)])
        )
    mixed = contribution(head)
    for part in got:
        mixed = mixed + part.astype(f32)
    return mixed.astype(bf16)


def solution(mesh):
    in_specs = (
        P("tok", "head"),
        P("tok", "head"),
        P("tok", "head"),
        P("head", None, None, None),
        P("tok", "head"),
        P("head", None),
    )
    out_specs = P("head", "tok")
    return jax.shard_map(
        on_device, mesh=mesh, in_specs=in_specs, out_specs=out_specs, check_vma=False
    )
```

```python
import jax
import jax.numpy as jnp
from jax import lax
from jax.experimental import pallas as pl
from jax.experimental.pallas import tpu as pltpu
from jax.sharding import PartitionSpec as P

NS_ITERS = 2


ns_a = 3.4445
ns_b = -4.775
ns_c = 2.0315
step_scale = 1.0
eps = 1e-07

f32 = jnp.float32
bf16 = jnp.bfloat16

NY, NZ, NC = 4, 8, 2
ROWS = 256


def chip_index(y, z, core):
    return (y * NZ + z) * NC + core


Y_GROUPS = [
    [chip_index(y, z, core) for y in range(NY)] for z in range(NZ) for core in range(NC)
]
Z_GROUPS = [
    [chip_index(y, z, core) for z in range(NZ)] for y in range(NY) for core in range(NC)
]
CORE_SWAP = [(device, device ^ 1) for device in range(NY * NZ * NC)]

SMEM = pl.BlockSpec(memory_space=pltpu.SMEM)
VMEM = pl.BlockSpec(memory_space=pltpu.VMEM)
ANY = pl.BlockSpec(memory_space=pl.ANY)


def swap_cores(array):
    return lax.ppermute(array, "tok", CORE_SWAP)


def exchange(blocks, groups):
    return lax.all_to_all(blocks, "tok", 0, 0, axis_index_groups=groups)


def sum_shares(blocks, groups):
    return jnp.sum(exchange(blocks, groups).astype(f32), axis=0).astype(bf16)


def gather_rows(rows, groups):
    size = len(groups[0])
    gathered = exchange(jnp.broadcast_to(rows[None], (size,) + rows.shape), groups)
    return gathered.reshape(-1, rows.shape[1])


def dot(left, right):
    return jnp.dot(left, right, preferred_element_type=f32)


def dot_nt(left, right):
    return lax.dot_general(left, right, (((1,), (1,)), ((), ())), preferred_element_type=f32)


def dot_tn(left, right):
    return lax.dot_general(left, right, (((0,), (0,)), ((), ())), preferred_element_type=f32)


def call(body, outs, in_specs, scratch, mib, flops, moved, name):
    return pl.pallas_call(
        body,
        out_shape=outs,
        in_specs=in_specs,
        scratch_shapes=scratch,
        compiler_params=pltpu.CompilerParams(vmem_limit_bytes=mib << 20),
        cost_estimate=pl.CostEstimate(flops=flops, bytes_accessed=moved, transcendentals=0),
        name=name,
    )


def shape(*dims, dtype=bf16):
    return jax.ShapeDtypeStruct(dims, dtype)


def gradients(core, keys, values, rates, weights):
    tokens, width = keys.shape
    half = width // 2

    def body(core_ref, k_ref, v_ref, r_ref, w_ref, own_send, shared_send, own_keep, shared_keep,
             hidden, errors, g_keep, g_send):
        first = core_ref[0] == 0
        for row in range(0, tokens, ROWS):
            rows = slice(row, row + ROWS)
            k = k_ref[rows, :]
            h1 = dot(k, w_ref[0, 0])
            h3 = dot(k, w_ref[0, 1])
            sig = jax.nn.sigmoid(h1)
            act = h1 * sig
            hidden[rows, :] = (act * h3).astype(bf16)
            e = (-r_ref[rows, :] * v_ref[rows, :].astype(f32)).astype(bf16)
            errors[rows, :] = e
            dz = dot_nt(e, w_ref[0, 2])
            g1 = (dz * h3 * (sig * (1.0 + h1 * (1.0 - sig)))).astype(bf16)
            g3 = (dz * act).astype(bf16)
            g_keep[rows, :] = jnp.where(first, g1, g3)
            g_send[rows, :] = jnp.where(first, g3, g1)
        own_send[...] = dot_tn(k_ref[...], g_send[...]).astype(bf16)
        own_keep[...] = dot_tn(k_ref[...], g_keep[...])
        left = dot_tn(hidden[...], errors[:, :half])
        right = dot_tn(hidden[...], errors[:, half:])
        shared_keep[...] = jnp.where(first, left, right)
        shared_send[...] = jnp.where(first, right, left).astype(bf16)

    return call(
        body,
        [
            shape(width, width),
            shape(width, half),
            shape(width, width, dtype=f32),
            shape(width, half, dtype=f32),
        ],
        [SMEM] + [VMEM] * 4,
        [pltpu.VMEM((tokens, width), bf16)] * 4,
        32,
        12 * tokens * width * width,
        12 * width * width,
        "gradients",
    )(core, keys, values, rates, weights)


def newton_schulz(x_ref, w_ref, out_ref, gram, poly, other):
    width = x_ref.shape[0]
    blocks = [slice(row, row + ROWS) for row in range(0, width, ROWS)]
    square_sum = jnp.zeros((1, 1), f32)
    for rows in blocks:
        wide = x_ref[rows, :].astype(f32)
        square_sum = square_sum + jnp.sum(wide * wide).reshape(1, 1)
    scale = 1.0 / (jnp.sqrt(square_sum) + eps)
    now = x_ref
    for turn in range(NS_ITERS):
        for rows in blocks:
            product = dot_nt(now[rows, :], now[...])
            if turn == 0:
                product = product * (scale * scale)
            gram[rows, :] = product.astype(bf16)
        for rows in blocks:
            squared = dot(gram[rows, :], gram[...])
            poly[rows, :] = (ns_b * gram[rows, :].astype(f32) + ns_c * squared).astype(bf16)
        for rows in blocks:
            new = ns_a * now[rows, :].astype(f32) + dot(poly[rows, :], now[...])
            if turn == 0:
                new = new * scale
            new = new.astype(bf16)
            if turn < NS_ITERS - 1:
                other[rows, :] = new
            else:
                step = step_scale * new.astype(f32)
                out_ref[rows, :] = (w_ref[rows, :].astype(f32) - step).astype(bf16)
        now = other


def own_step(core, summed, weights):
    width = weights.shape[-1]

    def body(core_ref, x_ref, w_hbm, out_ref, gram, poly, other, w_ref, sem):
        copy = pltpu.make_async_copy(w_hbm.at[0, core_ref[0]], w_ref, sem)
        copy.start()
        copy.wait()
        newton_schulz(x_ref, w_ref, out_ref, gram, poly, other)

    return call(
        body,
        shape(width, width),
        [SMEM, VMEM, ANY],
        [pltpu.VMEM((width, width), bf16)] * 4 + [pltpu.SemaphoreType.DMA],
        20,
        12 * width**3,
        6 * width * width,
        "own_step",
    )(core, summed, weights)


def shared_step(core, mine, partners, weights):
    width = weights.shape[-1]
    half = width // 2

    def body(core_ref, a_ref, b_ref, w_hbm, out_ref, gram, poly, other, x_ref, w_ref, sem):
        copy = pltpu.make_async_copy(w_hbm.at[0, 2], w_ref, sem)
        copy.start()
        first = core_ref[0] == 0
        x_ref[:, :half] = jnp.where(first, a_ref[...], b_ref[...])
        x_ref[:, half:] = jnp.where(first, b_ref[...], a_ref[...])
        copy.wait()
        newton_schulz(x_ref, w_ref, out_ref, gram, poly, other)

    return call(
        body,
        shape(width, width),
        [SMEM, VMEM, VMEM, ANY],
        [pltpu.VMEM((width, width), bf16)] * 5 + [pltpu.SemaphoreType.DMA],
        20,
        12 * width**3,
        6 * width * width,
        "shared_step",
    )(core, mine, partners, weights)


def project(place, queries, own, other, shared, out_proj):
    tokens, width = queries.shape
    heads = out_proj.shape[1] // width

    def body(place_ref, q_ref, own_ref, other_ref, shared_ref, p_hbm, *rest):
        outs, p_ref, sems = rest[:heads], rest[heads], rest[heads + 1]
        copies = []
        for step in range(heads):
            head = lax.rem(place_ref[1] + step, heads)
            start = pl.multiple_of(head * width, width)
            copies.append(
                pltpu.make_async_copy(
                    p_hbm.at[:, pl.ds(start, width)], p_ref.at[step], sems.at[step]
                )
            )
        for copy in copies:
            copy.start()
        first = place_ref[0] == 0
        q_own = dot(q_ref[...], own_ref[...])
        q_other = dot(q_ref[...], other_ref[...])
        q1 = jnp.where(first, q_own, q_other)
        q3 = jnp.where(first, q_other, q_own)
        gated = (q1 * jax.nn.sigmoid(q1) * q3).astype(bf16)
        outputs = dot(gated, shared_ref[...]).astype(bf16)
        for step in range(heads):
            copies[step].wait()
            outs[step][...] = dot(outputs, p_ref[step]).astype(outs[step].dtype)

    return call(
        body,
        [shape(tokens, width, dtype=f32)] + [shape(tokens, width)] * (heads - 1),
        [SMEM] + [VMEM] * 4 + [ANY],
        [pltpu.VMEM((heads, width, width), bf16), pltpu.SemaphoreType.DMA((heads,))],
        24,
        2 * tokens * width * width * (3 + heads),
        16 * width * width,
        "project",
    )(place, queries, own, other, shared, out_proj)


def mix(own, *got):
    tokens, width = own.shape

    def body(*refs):
        total = refs[0][...]
        for ref in refs[1:-1]:
            total = total + ref[...].astype(f32)
        refs[-1][...] = total.T.astype(bf16)

    return call(
        body, shape(width, tokens), [VMEM] * (1 + len(got)), [], 16, 0, 12 * tokens * width, "mix"
    )(own, *got)


def on_device(keys, values, rates, fast_weights, queries, out_proj):
    width = fast_weights.shape[-1]
    core = lax.axis_index("tok") % NC
    head = lax.axis_index("head")
    heads = lax.axis_size("head")
    place = jnp.stack([core, head]).astype(jnp.int32)

    own_send, shared_send, own_keep, shared_keep = gradients(
        place, keys, values, rates, fast_weights
    )
    shared_got = swap_cores(shared_send)
    own_got = swap_cores(own_send)
    chip_sum = jnp.concatenate(
        [own_keep + own_got.astype(f32), shared_keep + shared_got.astype(f32)], axis=1
    ).astype(bf16)

    y_sum = sum_shares(chip_sum.reshape(NY, width // NY, -1), Y_GROUPS)
    z_sum = sum_shares(y_sum.reshape(NZ, width // NY // NZ, -1), Z_GROUPS)
    summed = gather_rows(gather_rows(z_sum, Z_GROUPS), Y_GROUPS)

    shared_part = summed[:, width:]
    shared_other = swap_cores(shared_part)
    own_fresh = own_step(place, summed[:, :width], fast_weights)
    other_fresh = swap_cores(own_fresh)
    shared_fresh = shared_step(place, shared_part, shared_other, fast_weights)

    mixed, *parts = project(place, queries, own_fresh, other_fresh, shared_fresh, out_proj)
    got = [
        lax.ppermute(part, "head", [(i, (i + step) % heads) for i in range(heads)])
        for step, part in enumerate(parts, 1)
    ]
    return mix(mixed, *got)


def solution(mesh):
    in_specs = (
        P("tok", "head"),
        P("tok", "head"),
        P("tok", "head"),
        P("head", None, None, None),
        P("tok", "head"),
        P("head", None),
    )
    out_specs = P("head", "tok")
    return jax.shard_map(
        on_device, mesh=mesh, in_specs=in_specs, out_specs=out_specs, check_vma=False
    )
```

```python
import jax
import jax.numpy as jnp
from jax import lax
from jax.experimental import pallas as pl
from jax.experimental.pallas import tpu as pltpu
from jax.sharding import PartitionSpec as P

NS_ITERS = 2


ns_a = 3.4445
ns_b = -4.775
ns_c = 2.0315
step_scale = 1.0
eps = 1e-07

f32 = jnp.float32
bf16 = jnp.bfloat16

NY, NZ, NC = 4, 8, 2
ROWS = 256


def chip_index(y, z, core):
    return (y * NZ + z) * NC + core


Z_GROUPS = [
    [chip_index(y, z, core) for z in range(NZ)] for y in range(NY) for core in range(NC)
]
Y_UP = [(d, (d + NZ * NC) % (NY * NZ * NC)) for d in range(NY * NZ * NC)]
Y_DOWN = [(there, here) for here, there in Y_UP]
CORE_SWAP = [(device, device ^ 1) for device in range(NY * NZ * NC)]

SMEM = pl.BlockSpec(memory_space=pltpu.SMEM)
VMEM = pl.BlockSpec(memory_space=pltpu.VMEM)
ANY = pl.BlockSpec(memory_space=pl.ANY)


def swap_cores(array):
    return lax.ppermute(array, "tok", CORE_SWAP)


def exchange(blocks, groups):
    return lax.all_to_all(blocks, "tok", 0, 0, axis_index_groups=groups)


def sum_shares(blocks, groups):
    return jnp.sum(exchange(blocks, groups).astype(f32), axis=0).astype(bf16)


def gather_rows(rows, groups):
    size = len(groups[0])
    gathered = exchange(jnp.broadcast_to(rows[None], (size,) + rows.shape), groups)
    return gathered.reshape(-1, rows.shape[1])


def dot(left, right):
    return jnp.dot(left, right, preferred_element_type=f32)


def dot_nt(left, right):
    return lax.dot_general(left, right, (((1,), (1,)), ((), ())), preferred_element_type=f32)


def dot_tn(left, right):
    return lax.dot_general(left, right, (((0,), (0,)), ((), ())), preferred_element_type=f32)


def call(body, outs, in_specs, scratch, mib, flops, moved, name):
    return pl.pallas_call(
        body,
        out_shape=outs,
        in_specs=in_specs,
        scratch_shapes=scratch,
        compiler_params=pltpu.CompilerParams(vmem_limit_bytes=mib << 20),
        cost_estimate=pl.CostEstimate(flops=flops, bytes_accessed=moved, transcendentals=0),
        name=name,
    )


def shape(*dims, dtype=bf16):
    return jax.ShapeDtypeStruct(dims, dtype)


def gradients(place, keys, values, rates, weights):
    tokens, width = keys.shape
    half = width // 2
    lanes = rates.shape[1]

    def body(place_ref, r_ref, k_hbm, v_hbm, w_hbm, own_send, shared_send, own_keep, shared_keep,
             k_ref, v_ref, w_ref, hidden, errors, g_keep, g_send, sems):
        moves = [
            (k_hbm, k_ref),
            (w_hbm.at[0, 0], w_ref.at[0]),
            (w_hbm.at[0, 1], w_ref.at[1]),
            (v_hbm, v_ref),
            (w_hbm.at[0, 2], w_ref.at[2]),
        ]
        copies = [
            pltpu.make_async_copy(src, dst, sems.at[n]) for n, (src, dst) in enumerate(moves)
        ]
        for copy in copies:
            copy.start()
        first = place_ref[0] == 0
        rate_columns = r_ref[...].T
        copies[0].wait()
        copies[1].wait()
        for row in range(0, tokens, ROWS):
            rows = slice(row, row + ROWS)
            k = k_ref[rows, :]
            h1 = dot(k, w_ref[0])
            if row == 0:
                copies[2].wait()
            h3 = dot(k, w_ref[1])
            sig = jax.nn.sigmoid(h1)
            act = h1 * sig
            hidden[rows, :] = (act * h3).astype(bf16)
            if row == 0:
                copies[3].wait()
            for part in range(row, row + ROWS, lanes):
                rate = rate_columns[:, part // lanes : part // lanes + 1]
                span = slice(part, part + lanes)
                errors[span, :] = (-rate * v_ref[span, :].astype(f32)).astype(bf16)
            if row == 0:
                copies[4].wait()
            dz = dot_nt(errors[rows, :], w_ref[2])
            g1 = (dz * h3 * (sig * (1.0 + h1 * (1.0 - sig)))).astype(bf16)
            g3 = (dz * act).astype(bf16)
            g_keep[rows, :] = jnp.where(first, g1, g3)
            g_send[rows, :] = jnp.where(first, g3, g1)
        own_send[...] = dot_tn(k_ref[...], g_send[...]).astype(bf16)
        own_keep[...] = dot_tn(k_ref[...], g_keep[...])
        left = dot_tn(hidden[...], errors[:, :half])
        right = dot_tn(hidden[...], errors[:, half:])
        shared_keep[...] = jnp.where(first, left, right)
        shared_send[...] = jnp.where(first, right, left).astype(bf16)

    return call(
        body,
        [
            shape(width, width),
            shape(width, half),
            shape(width, width, dtype=f32),
            shape(width, half, dtype=f32),
        ],
        [SMEM, VMEM] + [ANY] * 3,
        [pltpu.VMEM((tokens, width), bf16)] * 2
        + [pltpu.VMEM((3, width, width), bf16)]
        + [pltpu.VMEM((tokens, width), bf16)] * 4
        + [pltpu.SemaphoreType.DMA((5,))],
        40,
        12 * tokens * width * width,
        12 * width * width,
        "gradients",
    )(place, rates, keys, values, weights)


def chip_sum(place, own_keep, own_got, shared_keep, shared_got):
    width, half = shared_keep.shape
    rows = width // NY
    wide = width + half

    def body(place_ref, ok_ref, og_ref, sk_ref, sg_ref, mine, *outs):
        for step in range(NY):
            start = lax.rem(place_ref[2] + step, NY) * rows
            for part in range(2):
                cut = rows // 2
                span = pl.ds(pl.multiple_of(start + part * cut, cut), cut)
                own = ok_ref[span, :] + og_ref[span, :].astype(f32)
                shared = sk_ref[span, :] + sg_ref[span, :].astype(f32)
                if step == 0:
                    mine[part * cut : (part + 1) * cut, :width] = own
                    mine[part * cut : (part + 1) * cut, width:] = shared
                else:
                    out = outs[2 * (step - 1) + part]
                    out[:, :width] = own.astype(bf16)
                    out[:, width:] = shared.astype(bf16)

    return call(
        body,
        [shape(rows, wide, dtype=f32)] + [shape(rows // 2, wide)] * (2 * NY - 2),
        [SMEM] + [VMEM] * 4,
        [],
        16,
        0,
        10 * width * wide,
        "chip_sum",
    )(place, own_keep, own_got, shared_keep, shared_got)


def assemble(place, own, previous, following, opposite):
    rows, wide = own.shape
    width = rows * NY
    pieces = [own, *following, *opposite, *previous]

    def body(place_ref, own_ref, *rest):
        parts, (x_ref, s_ref) = rest[:-2], rest[-2:]
        base = place_ref[2]
        start = pl.multiple_of(base * rows, rows)
        x_ref[pl.ds(start, rows), :] = own_ref[:, :width]
        s_ref[pl.ds(start, rows), :] = own_ref[:, width:]
        for n, part in enumerate(parts):
            cut = rows // 2
            start = lax.rem(base + 1 + n // 2, NY) * rows + (n % 2) * cut
            span = pl.ds(pl.multiple_of(start, cut), cut)
            x_ref[span, :] = part[:, :width]
            s_ref[span, :] = part[:, width:]

    return call(
        body,
        [shape(width, width), shape(width, wide - width)],
        [SMEM] + [VMEM] * len(pieces),
        [],
        16,
        0,
        4 * width * wide,
        "assemble",
    )(place, *pieces)


def newton_schulz(x_ref, w_ref, out_ref, gram, poly, other):
    width = x_ref.shape[0]
    blocks = [slice(row, row + ROWS) for row in range(0, width, ROWS)]
    square_sum = jnp.zeros((1, 1), f32)
    for rows in blocks:
        wide = x_ref[rows, :].astype(f32)
        square_sum = square_sum + jnp.sum(wide * wide).reshape(1, 1)
    scale = 1.0 / (jnp.sqrt(square_sum) + eps)
    now = x_ref
    for turn in range(NS_ITERS):
        for rows in blocks:
            product = dot_nt(now[rows, :], now[...])
            if turn == 0:
                product = product * (scale * scale)
            gram[rows, :] = product.astype(bf16)
        for rows in blocks:
            squared = dot(gram[rows, :], gram[...])
            poly[rows, :] = (ns_b * gram[rows, :].astype(f32) + ns_c * squared).astype(bf16)
        for rows in blocks:
            new = ns_a * now[rows, :].astype(f32) + dot(poly[rows, :], now[...])
            if turn == 0:
                new = new * scale
            new = new.astype(bf16)
            if turn < NS_ITERS - 1:
                other[rows, :] = new
            else:
                step = step_scale * new.astype(f32)
                out_ref[rows, :] = (w_ref[rows, :].astype(f32) - step).astype(bf16)
        now = other


def own_step(core, summed, weights):
    width = weights.shape[-1]

    def body(core_ref, x_ref, w_hbm, out_ref, gram, poly, other, w_ref, sem):
        copy = pltpu.make_async_copy(w_hbm.at[0, core_ref[0]], w_ref, sem)
        copy.start()
        copy.wait()
        newton_schulz(x_ref, w_ref, out_ref, gram, poly, other)

    return call(
        body,
        shape(width, width),
        [SMEM, VMEM, ANY],
        [pltpu.VMEM((width, width), bf16)] * 4 + [pltpu.SemaphoreType.DMA],
        20,
        12 * width**3,
        6 * width * width,
        "own_step",
    )(core, summed, weights)


def shared_step(core, mine, partners, weights):
    width = weights.shape[-1]
    half = width // 2

    def body(core_ref, a_ref, b_ref, w_hbm, out_ref, gram, poly, other, x_ref, w_ref, sem):
        copy = pltpu.make_async_copy(w_hbm.at[0, 2], w_ref, sem)
        copy.start()
        first = core_ref[0] == 0
        x_ref[:, :half] = jnp.where(first, a_ref[...], b_ref[...])
        x_ref[:, half:] = jnp.where(first, b_ref[...], a_ref[...])
        copy.wait()
        newton_schulz(x_ref, w_ref, out_ref, gram, poly, other)

    return call(
        body,
        shape(width, width),
        [SMEM, VMEM, VMEM, ANY],
        [pltpu.VMEM((width, width), bf16)] * 5 + [pltpu.SemaphoreType.DMA],
        20,
        12 * width**3,
        6 * width * width,
        "shared_step",
    )(core, mine, partners, weights)


def project(place, queries, own, other, shared, out_proj):
    tokens, width = queries.shape
    heads = out_proj.shape[1] // width

    def body(place_ref, q_ref, own_ref, other_ref, shared_ref, p_hbm, *rest):
        outs, p_ref, sems = rest[:-2], rest[-2], rest[-1]
        copies = []
        for step in range(heads):
            head = lax.rem(place_ref[1] + step, heads)
            start = pl.multiple_of(head * width, width)
            copies.append(
                pltpu.make_async_copy(
                    p_hbm.at[:, pl.ds(start, width)], p_ref.at[step], sems.at[step]
                )
            )
        for copy in copies:
            copy.start()
        first = place_ref[0] == 0
        q_own = dot(q_ref[...], own_ref[...])
        q_other = dot(q_ref[...], other_ref[...])
        q1 = jnp.where(first, q_own, q_other)
        q3 = jnp.where(first, q_other, q_own)
        gated = (q1 * jax.nn.sigmoid(q1) * q3).astype(bf16)
        outputs = dot(gated, shared_ref[...]).astype(bf16)
        cut = tokens // 2
        for step in range(heads):
            copies[step].wait()
            product = dot(outputs, p_ref[step])
            if step == 0:
                outs[0][...] = product
            else:
                outs[2 * step - 1][...] = product[:cut].astype(bf16)
                outs[2 * step][...] = product[cut:].astype(bf16)

    return call(
        body,
        [shape(tokens, width, dtype=f32)] + [shape(tokens // 2, width)] * (2 * heads - 2),
        [SMEM] + [VMEM] * 4 + [ANY],
        [pltpu.VMEM((heads, width, width), bf16), pltpu.SemaphoreType.DMA((heads,))],
        24,
        2 * tokens * width * width * (3 + heads),
        16 * width * width,
        "project",
    )(place, queries, own, other, shared, out_proj)


def mix(own, top, bottom):
    tokens, width = own.shape
    cut = tokens // 2
    count = len(top)

    def body(own_ref, *rest):
        out = rest[-1]
        for part in range(2):
            total = own_ref[part * cut : (part + 1) * cut, :]
            for ref in rest[part * count : (part + 1) * count]:
                total = total + ref[...].astype(f32)
            out[:, part * cut : (part + 1) * cut] = total.T.astype(bf16)

    return call(
        body,
        shape(width, tokens),
        [VMEM] * (1 + 2 * count),
        [],
        16,
        0,
        12 * tokens * width,
        "mix",
    )(own, *top, *bottom)


def shift(array, axis, pairs):
    return lax.ppermute(array, axis, pairs)


def add(left, right):
    return (left.astype(f32) + right.astype(f32)).astype(bf16)


def ring_sum(pieces, axis, up, down):
    next_a, next_b, far_a, far_b, previous_a, previous_b = pieces
    relay_a = shift(far_a, axis, up)
    relay_b = shift(far_b, axis, down)
    from_down_b = shift(next_b, axis, up)
    from_up_a = shift(previous_a, axis, down)
    from_down_a = shift(add(next_a, relay_a), axis, up)
    from_up_b = shift(add(previous_b, relay_b), axis, down)
    return [from_down_a, from_up_a], [from_down_b, from_up_b]


def ring_gather(block, axis, up, down):
    cut = block.shape[0] // 2
    block_a, block_b = block[:cut], block[cut:]
    previous_a = shift(block_a, axis, up)
    following_b = shift(block_b, axis, down)
    previous_b = shift(block_b, axis, up)
    following_a = shift(block_a, axis, down)
    far_a = shift(previous_a, axis, up)
    far_b = shift(following_b, axis, down)
    return (previous_a, previous_b), (following_a, following_b), (far_a, far_b)


def on_device(keys, values, rates, fast_weights, queries, out_proj):
    width = fast_weights.shape[-1]
    place_in_tok = lax.axis_index("tok")
    core = place_in_tok % NC
    head = lax.axis_index("head")
    heads = lax.axis_size("head")
    place = jnp.stack([core, head, place_in_tok // (NC * NZ)]).astype(jnp.int32)

    own_send, shared_send, own_keep, shared_keep = gradients(
        place, keys, values, rates.reshape(-1, 128), fast_weights
    )
    own_got = swap_cores(own_send)
    shared_got = swap_cores(shared_send)
    mine, *shares = chip_sum(place, own_keep, own_got, shared_keep, shared_got)

    got_a, got_b = ring_sum(shares, "tok", Y_UP, Y_DOWN)
    cut = mine.shape[0] // 2
    first_half = mine[:cut] + got_a[0].astype(f32) + got_a[1].astype(f32)
    second_half = mine[cut:] + got_b[0].astype(f32) + got_b[1].astype(f32)
    y_sum = jnp.concatenate([first_half, second_half]).astype(bf16)
    z_sum = sum_shares(y_sum.reshape(NZ, width // NY // NZ, -1), Z_GROUPS)
    y_rows = gather_rows(z_sum, Z_GROUPS)
    previous, following, far = ring_gather(y_rows, "tok", Y_UP, Y_DOWN)
    own_sum, shared_part = assemble(place, y_rows, previous, following, far)

    shared_other = swap_cores(shared_part)
    own_fresh = own_step(place, own_sum, fast_weights)
    other_fresh = swap_cores(own_fresh)
    shared_fresh = shared_step(place, shared_part, shared_other, fast_weights)

    mixed, *shares = project(place, queries, own_fresh, other_fresh, shared_fresh, out_proj)
    up = [(i, (i + 1) % heads) for i in range(heads)]
    down = [(i, (i - 1) % heads) for i in range(heads)]
    return mix(mixed, *ring_sum(shares, "head", up, down))


def solution(mesh):
    in_specs = (
        P("tok", "head"),
        P("tok", "head"),
        P("tok", "head"),
        P("head", None, None, None),
        P("tok", "head"),
        P("head", None),
    )
    out_specs = P("head", "tok")
    return jax.shard_map(
        on_device, mesh=mesh, in_specs=in_specs, out_specs=out_specs, check_vma=False
    )
```

```python
import jax
import jax.numpy as jnp
from jax import lax
from jax.experimental import pallas as pl
from jax.experimental.pallas import tpu as pltpu
from jax.sharding import PartitionSpec as P

NS_ITERS = 2


ns_a = 3.4445
ns_b = -4.775
ns_c = 2.0315
step_scale = 1.0
eps = 1e-07

f32 = jnp.float32
bf16 = jnp.bfloat16

NY, NZ, NC = 4, 8, 2
ROWS = 256


def chip_index(y, z, core):
    return (y * NZ + z) * NC + core


Z_GROUPS = [
    [chip_index(y, z, core) for z in range(NZ)] for y in range(NY) for core in range(NC)
]
Y_UP = [(d, (d + NZ * NC) % (NY * NZ * NC)) for d in range(NY * NZ * NC)]
Y_DOWN = [(there, here) for here, there in Y_UP]
CORE_SWAP = [(device, device ^ 1) for device in range(NY * NZ * NC)]

SMEM = pl.BlockSpec(memory_space=pltpu.SMEM)
VMEM = pl.BlockSpec(memory_space=pltpu.VMEM)
HBM = pl.BlockSpec(memory_space=pltpu.HBM)


def swap_cores(array):
    return lax.ppermute(array, "tok", CORE_SWAP)


def exchange(blocks, groups):
    return lax.all_to_all(blocks, "tok", 0, 0, axis_index_groups=groups)


def sum_shares(blocks, groups):
    return jnp.sum(exchange(blocks, groups).astype(f32), axis=0).astype(bf16)


def gather_rows(rows, groups):
    size = len(groups[0])
    gathered = exchange(jnp.broadcast_to(rows[None], (size,) + rows.shape), groups)
    return gathered.reshape(-1, rows.shape[1])


def dot(left, right):
    return jnp.dot(left, right, preferred_element_type=f32)


def dot_nt(left, right):
    return lax.dot_general(left, right, (((1,), (1,)), ((), ())), preferred_element_type=f32)


def dot_tn(left, right):
    return lax.dot_general(left, right, (((0,), (0,)), ((), ())), preferred_element_type=f32)


def call(body, outs, in_specs, scratch, mib, flops, moved, name, out_specs=None):
    if out_specs is None:
        out_specs = [VMEM] * len(outs) if isinstance(outs, list) else VMEM
    return pl.pallas_call(
        body,
        out_shape=outs,
        in_specs=in_specs,
        out_specs=out_specs,
        scratch_shapes=scratch,
        compiler_params=pltpu.CompilerParams(vmem_limit_bytes=mib << 20),
        cost_estimate=pl.CostEstimate(flops=flops, bytes_accessed=moved, transcendentals=0),
        name=name,
    )


def shape(*dims, dtype=bf16):
    return jax.ShapeDtypeStruct(dims, dtype)


def gradients(place, keys, values, rates, weights):
    tokens, width = keys.shape
    half = width // 2
    lanes = rates.shape[1]

    def body(place_ref, r_ref, k_hbm, v_hbm, w_hbm, *rest):
        outs, refs = rest[:5], rest[5:10]
        k_ref, v_ref, w_ref, errors, g_send, sems, out_sems = rest[10:]
        own_send, shared_send, g_keep, hidden, e_keep = refs
        stores = [
            pltpu.make_async_copy(ref, out, out_sems.at[n])
            for n, (ref, out) in enumerate(zip(refs, outs))
        ]
        moves = [
            (k_hbm, k_ref),
            (w_hbm.at[0, 0], w_ref.at[0]),
            (w_hbm.at[0, 1], w_ref.at[1]),
            (v_hbm, v_ref),
            (w_hbm.at[0, 2], w_ref.at[2]),
        ]
        copies = [
            pltpu.make_async_copy(src, dst, sems.at[n]) for n, (src, dst) in enumerate(moves)
        ]
        for copy in copies:
            copy.start()
        first = place_ref[0] == 0
        rate_columns = r_ref[...].T
        copies[0].wait()
        copies[1].wait()
        for row in range(0, tokens, ROWS):
            rows = slice(row, row + ROWS)
            k = k_ref[rows, :]
            h1 = dot(k, w_ref[0])
            if row == 0:
                copies[2].wait()
            h3 = dot(k, w_ref[1])
            sig = jax.nn.sigmoid(h1)
            act = h1 * sig
            hidden[rows, :] = (act * h3).astype(bf16)
            if row == 0:
                copies[3].wait()
            for part in range(row, row + ROWS, lanes):
                rate = rate_columns[:, part // lanes : part // lanes + 1]
                span = slice(part, part + lanes)
                errors[span, :] = (-rate * v_ref[span, :].astype(f32)).astype(bf16)
            if row == 0:
                copies[4].wait()
            dz = dot_nt(errors[rows, :], w_ref[2])
            g1 = (dz * h3 * (sig * (1.0 + h1 * (1.0 - sig)))).astype(bf16)
            g3 = (dz * act).astype(bf16)
            g_keep[rows, :] = jnp.where(first, g1, g3)
            g_send[rows, :] = jnp.where(first, g3, g1)
        left = errors[:, :half]
        right = errors[:, half:]
        e_keep[...] = jnp.where(first, left, right)
        for store in stores[2:]:
            store.start()
        own_send[...] = dot_tn(k_ref[...], g_send[...]).astype(bf16)
        stores[0].start()
        shared_send[...] = dot_tn(hidden[...], jnp.where(first, right, left)).astype(bf16)
        stores[1].start()
        for store in stores:
            store.wait()

    results = [(width, width), (width, half), (tokens, width), (tokens, width), (tokens, half)]
    return call(
        body,
        [shape(*dims) for dims in results],
        [SMEM, VMEM] + [HBM] * 3,
        [pltpu.VMEM(dims, bf16) for dims in results]
        + [pltpu.VMEM((tokens, width), bf16)] * 2
        + [pltpu.VMEM((3, width, width), bf16)]
        + [pltpu.VMEM((tokens, width), bf16)] * 2
        + [pltpu.SemaphoreType.DMA((5,))] * 2,
        60,
        9 * tokens * width * width,
        12 * width * width,
        "gradients",
        [HBM] * len(results),
    )(place, rates, keys, values, weights)


def keep(keys, g_keep, hidden, e_keep):
    width, half = hidden.shape[1], e_keep.shape[1]

    def body(k_ref, g_ref, h_ref, e_ref, own, shared):
        own[...] = dot_tn(k_ref[...], g_ref[...])
        shared[...] = dot_tn(h_ref[...], e_ref[...])

    return call(
        body,
        [shape(width, width, dtype=f32), shape(width, half, dtype=f32)],
        [VMEM] * 4,
        [],
        16,
        3 * keys.shape[0] * width * width,
        9 * width * width,
        "keep",
    )(keys, g_keep, hidden, e_keep)


def chip_sum(place, own_keep, own_got, shared_keep, shared_got):
    width, half = shared_keep.shape
    rows = width // NY
    wide = width + half

    def body(place_ref, ok_ref, og_ref, sk_ref, sg_ref, mine, *outs):
        for step in range(NY):
            start = lax.rem(place_ref[2] + step, NY) * rows
            for part in range(2):
                cut = rows // 2
                span = pl.ds(pl.multiple_of(start + part * cut, cut), cut)
                own = ok_ref[span, :] + og_ref[span, :].astype(f32)
                shared = sk_ref[span, :] + sg_ref[span, :].astype(f32)
                if step == 0:
                    mine[part * cut : (part + 1) * cut, :width] = own
                    mine[part * cut : (part + 1) * cut, width:] = shared
                else:
                    out = outs[2 * (step - 1) + part]
                    out[:, :width] = own.astype(bf16)
                    out[:, width:] = shared.astype(bf16)

    return call(
        body,
        [shape(rows, wide, dtype=f32)] + [shape(rows // 2, wide)] * (2 * NY - 2),
        [SMEM] + [VMEM] * 4,
        [],
        16,
        0,
        10 * width * wide,
        "chip_sum",
    )(place, own_keep, own_got, shared_keep, shared_got)


def assemble(place, own, previous, following, opposite):
    rows, wide = own.shape
    width = rows * NY
    pieces = [own, *following, *opposite, *previous]

    def body(place_ref, own_ref, *rest):
        parts, (x_ref, s_ref) = rest[:-2], rest[-2:]
        base = place_ref[2]
        start = pl.multiple_of(base * rows, rows)
        x_ref[pl.ds(start, rows), :] = own_ref[:, :width]
        s_ref[pl.ds(start, rows), :] = own_ref[:, width:]
        for n, part in enumerate(parts):
            cut = rows // 2
            start = lax.rem(base + 1 + n // 2, NY) * rows + (n % 2) * cut
            span = pl.ds(pl.multiple_of(start, cut), cut)
            x_ref[span, :] = part[:, :width]
            s_ref[span, :] = part[:, width:]

    return call(
        body,
        [shape(width, width), shape(width, wide - width)],
        [SMEM] + [VMEM] * len(pieces),
        [],
        16,
        0,
        4 * width * wide,
        "assemble",
    )(place, *pieces)


def newton_schulz(x_ref, w_ref, w_copy, outs, gram, poly, other):
    width = x_ref.shape[0]
    blocks = [slice(row, row + ROWS) for row in range(0, width, ROWS)]

    def store(ref, n, below):
        rows = blocks[n]
        ref[rows, : rows.stop] = below
        for column in blocks[:n]:
            ref[column, rows] = below[:, column].T

    square_sum = jnp.zeros((1, 1), f32)
    for rows in blocks:
        wide = x_ref[rows, :].astype(f32)
        square_sum = square_sum + jnp.sum(wide * wide).reshape(1, 1)
    scale = 1.0 / (jnp.sqrt(square_sum) + eps)
    now = x_ref
    for turn in range(NS_ITERS):
        for n, rows in enumerate(blocks):
            product = dot_nt(now[rows, :], now[: rows.stop, :])
            if turn == 0:
                product = product * (scale * scale)
            store(gram, n, product.astype(bf16))
        for n, rows in enumerate(blocks):
            squared = dot(gram[rows, :], gram[:, : rows.stop])
            linear = gram[rows, : rows.stop].astype(f32)
            store(poly, n, (ns_b * linear + ns_c * squared).astype(bf16))
        if turn == NS_ITERS - 1:
            w_copy.wait()
        for rows in blocks:
            new = ns_a * now[rows, :].astype(f32) + dot(poly[rows, :], now[...])
            if turn == 0:
                new = new * scale
            new = new.astype(bf16)
            if turn < NS_ITERS - 1:
                other[rows, :] = new
            else:
                step = step_scale * new.astype(f32)
                fresh = (w_ref[rows, :].astype(f32) - step).astype(bf16)
                for n, out in enumerate(outs):
                    height = out.shape[0]
                    start, stop = max(rows.start, n * height), min(rows.stop, (n + 1) * height)
                    if start < stop:
                        inside = slice(start - n * height, stop - n * height)
                        out[inside, :] = fresh[start - rows.start : stop - rows.start]
        now = other


def own_step(core, summed, weights):
    width = weights.shape[-1]

    def body(core_ref, x_ref, w_hbm, top, bottom, gram, poly, other, w_ref, sem):
        copy = pltpu.make_async_copy(w_hbm.at[0, core_ref[0]], w_ref, sem)
        copy.start()
        newton_schulz(x_ref, w_ref, copy, (top, bottom), gram, poly, other)

    return call(
        body,
        [shape(width // 2, width)] * 2,
        [SMEM, VMEM, HBM],
        [pltpu.VMEM((width, width), bf16)] * 4 + [pltpu.SemaphoreType.DMA],
        20,
        10 * width**3,
        6 * width * width,
        "own_step",
    )(core, summed, weights)


def shared_step(core, mine, partners, weights):
    width = weights.shape[-1]
    half = width // 2

    def body(core_ref, a_ref, b_ref, w_hbm, out_ref, gram, poly, other, x_ref, w_ref, sem):
        copy = pltpu.make_async_copy(w_hbm.at[0, 2], w_ref, sem)
        copy.start()
        first = core_ref[0] == 0
        x_ref[:, :half] = jnp.where(first, a_ref[...], b_ref[...])
        x_ref[:, half:] = jnp.where(first, b_ref[...], a_ref[...])
        newton_schulz(x_ref, w_ref, copy, (out_ref,), gram, poly, other)

    return call(
        body,
        shape(width, width),
        [SMEM, VMEM, VMEM, HBM],
        [pltpu.VMEM((width, width), bf16)] * 5 + [pltpu.SemaphoreType.DMA],
        20,
        10 * width**3,
        6 * width * width,
        "shared_step",
    )(core, mine, partners, weights)


def project(place, queries, own, other, shared, out_proj):
    tokens, width = queries.shape
    heads = out_proj.shape[1] // width

    half = width // 2

    def body(place_ref, q_ref, own_a, own_b, other_a, other_b, shared_ref, p_ref, *outs):
        first = place_ref[0] == 0
        left, right = q_ref[:, :half], q_ref[:, half:]
        q_own = dot(left, own_a[...]) + dot(right, own_b[...])
        q_other = dot(left, other_a[...]) + dot(right, other_b[...])
        q1 = jnp.where(first, q_own, q_other)
        q3 = jnp.where(first, q_other, q_own)
        gated = (q1 * jax.nn.sigmoid(q1) * q3).astype(bf16)
        outputs = dot(gated, shared_ref[...]).astype(bf16)
        cut = tokens // 2
        for step in range(heads):
            head = lax.rem(place_ref[1] + step, heads)
            start = pl.multiple_of(head * width, width)
            product = dot(outputs, p_ref[:, pl.ds(start, width)])
            if step == 0:
                outs[0][...] = product
            else:
                outs[2 * step - 1][...] = product[:cut].astype(bf16)
                outs[2 * step][...] = product[cut:].astype(bf16)

    return call(
        body,
        [shape(tokens, width, dtype=f32)] + [shape(tokens // 2, width)] * (2 * heads - 2),
        [SMEM] + [VMEM] * 7,
        [],
        20,
        2 * tokens * width * width * (3 + heads),
        16 * width * width,
        "project",
    )(place, queries, *own, *other, shared, out_proj)


def mix(own, top, bottom):
    tokens, width = own.shape
    cut = tokens // 2
    count = len(top)

    def body(own_ref, *rest):
        out = rest[-1]
        for part in range(2):
            total = own_ref[part * cut : (part + 1) * cut, :]
            for ref in rest[part * count : (part + 1) * count]:
                total = total + ref[...].astype(f32)
            out[:, part * cut : (part + 1) * cut] = total.T.astype(bf16)

    return call(
        body,
        shape(width, tokens),
        [VMEM] * (1 + 2 * count),
        [],
        16,
        0,
        12 * tokens * width,
        "mix",
    )(own, *top, *bottom)


def shift(array, axis, pairs):
    return lax.ppermute(array, axis, pairs)


def add(left, right):
    return (left.astype(f32) + right.astype(f32)).astype(bf16)


def ring_sum(pieces, axis, up, down):
    next_a, next_b, far_a, far_b, previous_a, previous_b = pieces
    relay_a = shift(far_a, axis, up)
    relay_b = shift(far_b, axis, down)
    from_down_b = shift(next_b, axis, up)
    from_up_a = shift(previous_a, axis, down)
    from_down_a = shift(add(next_a, relay_a), axis, up)
    from_up_b = shift(add(previous_b, relay_b), axis, down)
    return [from_down_a, from_up_a], [from_down_b, from_up_b]


def ring_gather(block, axis, up, down):
    cut = block.shape[0] // 2
    block_a, block_b = block[:cut], block[cut:]
    previous_a = shift(block_a, axis, up)
    following_b = shift(block_b, axis, down)
    previous_b = shift(block_b, axis, up)
    following_a = shift(block_a, axis, down)
    far_a = shift(previous_a, axis, up)
    far_b = shift(following_b, axis, down)
    return (previous_a, previous_b), (following_a, following_b), (far_a, far_b)


def on_device(keys, values, rates, fast_weights, queries, out_proj):
    width = fast_weights.shape[-1]
    place_in_tok = lax.axis_index("tok")
    core = place_in_tok % NC
    head = lax.axis_index("head")
    heads = lax.axis_size("head")
    place = jnp.stack([core, head, place_in_tok // (NC * NZ)]).astype(jnp.int32)

    own_send, shared_send, g_keep, hidden, e_keep = gradients(
        place, keys, values, rates.reshape(-1, 128), fast_weights
    )
    own_got = swap_cores(own_send)
    shared_got = swap_cores(shared_send)
    own_keep, shared_keep = keep(keys, g_keep, hidden, e_keep)
    mine, *shares = chip_sum(place, own_keep, own_got, shared_keep, shared_got)

    got_a, got_b = ring_sum(shares, "tok", Y_UP, Y_DOWN)
    cut = mine.shape[0] // 2
    first_half = mine[:cut] + got_a[0].astype(f32) + got_a[1].astype(f32)
    second_half = mine[cut:] + got_b[0].astype(f32) + got_b[1].astype(f32)
    y_sum = jnp.concatenate([first_half, second_half]).astype(bf16)
    z_sum = sum_shares(y_sum.reshape(NZ, width // NY // NZ, -1), Z_GROUPS)
    y_rows = gather_rows(z_sum, Z_GROUPS)
    previous, following, far = ring_gather(y_rows, "tok", Y_UP, Y_DOWN)
    own_sum, shared_part = assemble(place, y_rows, previous, following, far)

    shared_other = swap_cores(shared_part)
    own_fresh = own_step(place, own_sum, fast_weights)
    other_fresh = [swap_cores(rows) for rows in own_fresh]
    shared_fresh = shared_step(place, shared_part, shared_other, fast_weights)

    mixed, *shares = project(place, queries, own_fresh, other_fresh, shared_fresh, out_proj)
    up = [(i, (i + 1) % heads) for i in range(heads)]
    down = [(i, (i - 1) % heads) for i in range(heads)]
    return mix(mixed, *ring_sum(shares, "head", up, down))


def solution(mesh):
    in_specs = (
        P("tok", "head"),
        P("tok", "head"),
        P("tok", "head"),
        P("head", None, None, None),
        P("tok", "head"),
        P("head", None),
    )
    out_specs = P("head", "tok")
    return jax.shard_map(
        on_device, mesh=mesh, in_specs=in_specs, out_specs=out_specs, check_vma=False
    )
```

```python
import jax
import jax.numpy as jnp
from jax import lax
from jax.experimental import pallas as pl
from jax.experimental.pallas import tpu as pltpu
from jax.sharding import PartitionSpec as P

NS_ITERS = 2


ns_a = 3.4445
ns_b = -4.775
ns_c = 2.0315
step_scale = 1.0
eps = 1e-07

f32 = jnp.float32
bf16 = jnp.bfloat16

NY, NZ, NC = 4, 8, 2
ROWS = 256


def chip_index(y, z, core):
    return (y * NZ + z) * NC + core


Z_GROUPS = [
    [chip_index(y, z, core) for z in range(NZ)] for y in range(NY) for core in range(NC)
]
Y_UP = [(d, (d + NZ * NC) % (NY * NZ * NC)) for d in range(NY * NZ * NC)]
Y_DOWN = [(there, here) for here, there in Y_UP]
CORE_SWAP = [(device, device ^ 1) for device in range(NY * NZ * NC)]

VMEM = pl.BlockSpec(memory_space=pltpu.VMEM)
HBM = pl.BlockSpec(memory_space=pltpu.HBM)


def swap_cores(array):
    return lax.ppermute(array, "tok", CORE_SWAP)


def exchange(blocks, groups):
    return lax.all_to_all(blocks, "tok", 0, 0, axis_index_groups=groups)


def sum_shares(blocks, groups):
    return jnp.sum(exchange(blocks, groups).astype(f32), axis=0).astype(bf16)


def gather_rows(rows, groups):
    size = len(groups[0])
    gathered = exchange(jnp.broadcast_to(rows[None], (size,) + rows.shape), groups)
    return gathered.reshape(-1, rows.shape[1])


def dot(left, right):
    return jnp.dot(left, right, preferred_element_type=f32)


def dot_nt(left, right):
    return lax.dot_general(left, right, (((1,), (1,)), ((), ())), preferred_element_type=f32)


def dot_tn(left, right):
    return lax.dot_general(left, right, (((0,), (0,)), ((), ())), preferred_element_type=f32)


def call(body, outs, in_specs, scratch, mib, flops, moved, name, out_specs=None):
    if out_specs is None:
        out_specs = [VMEM] * len(outs) if isinstance(outs, list) else VMEM
    return pl.pallas_call(
        body,
        out_shape=outs,
        in_specs=in_specs,
        out_specs=out_specs,
        scratch_shapes=scratch,
        compiler_params=pltpu.CompilerParams(vmem_limit_bytes=mib << 20),
        cost_estimate=pl.CostEstimate(flops=flops, bytes_accessed=moved, transcendentals=0),
        name=name,
    )


def own_core():
    return lax.rem(lax.axis_index("tok"), NC)


def own_y():
    return lax.div(lax.axis_index("tok"), NZ * NC)


def shape(*dims, dtype=bf16):
    return jax.ShapeDtypeStruct(dims, dtype)


def gradients(keys, values, rates, weights):
    tokens, width = keys.shape
    half = width // 2
    lanes = rates.shape[1]

    def body(r_ref, k_hbm, v_hbm, w_hbm, *rest):
        outs, refs = rest[:3], rest[3:6]
        k_ref, v_ref, w_ref, errors, g_send, sems, out_sems = rest[6:]
        own_send, shared_send, factors = refs
        g_keep, hidden = factors.at[:, :width], factors.at[:, width : 2 * width]
        stores = [
            pltpu.make_async_copy(ref, out, out_sems.at[n])
            for n, (ref, out) in enumerate(zip(refs, outs))
        ]
        moves = [
            (k_hbm, k_ref),
            (w_hbm.at[0, 0], w_ref.at[0]),
            (w_hbm.at[0, 1], w_ref.at[1]),
            (v_hbm, v_ref),
            (w_hbm.at[0, 2], w_ref.at[2]),
        ]
        copies = [
            pltpu.make_async_copy(src, dst, sems.at[n]) for n, (src, dst) in enumerate(moves)
        ]
        for copy in copies:
            copy.start()
        first = own_core() == 0
        rate_columns = r_ref[...].T
        copies[0].wait()
        copies[1].wait()
        for row in range(0, tokens, ROWS):
            rows = slice(row, row + ROWS)
            k = k_ref[rows, :]
            h1 = dot(k, w_ref[0])
            if row == 0:
                copies[2].wait()
            h3 = dot(k, w_ref[1])
            sig = jax.nn.sigmoid(h1)
            act = h1 * sig
            hidden[rows, :] = (act * h3).astype(bf16)
            if row == 0:
                copies[3].wait()
            for part in range(row, row + ROWS, lanes):
                rate = rate_columns[:, part // lanes : part // lanes + 1]
                span = slice(part, part + lanes)
                errors[span, :] = (-rate * v_ref[span, :].astype(f32)).astype(bf16)
            if row == 0:
                copies[4].wait()
            dz = dot_nt(errors[rows, :], w_ref[2])
            g1 = (dz * h3 * (sig * (1.0 + h1 * (1.0 - sig)))).astype(bf16)
            g3 = (dz * act).astype(bf16)
            g_keep[rows, :] = jnp.where(first, g1, g3)
            g_send[rows, :] = jnp.where(first, g3, g1)
        left = errors[:, :half]
        right = errors[:, half:]
        factors[:, 2 * width :] = jnp.where(first, left, right)
        stores[2].start()
        own_send[...] = dot_tn(k_ref[...], g_send[...]).astype(bf16)
        stores[0].start()
        shared_send[...] = dot_tn(hidden[...], jnp.where(first, right, left)).astype(bf16)
        stores[1].start()
        for store in stores:
            store.wait()

    results = [(width, width), (width, half), (tokens, 2 * width + half)]
    return call(
        body,
        [shape(*dims) for dims in results],
        [VMEM] + [HBM] * 3,
        [pltpu.VMEM(dims, bf16) for dims in results]
        + [pltpu.VMEM((tokens, width), bf16)] * 2
        + [pltpu.VMEM((3, width, width), bf16)]
        + [pltpu.VMEM((tokens, width), bf16)] * 2
        + [pltpu.SemaphoreType.DMA((5,)), pltpu.SemaphoreType.DMA((3,))],
        60,
        9 * tokens * width * width,
        12 * width * width,
        "gradients",
        [HBM] * len(results),
    )(rates, keys, values, weights)


def keep(keys, factors):
    width = keys.shape[1]
    half = width // 2

    def body(k_ref, f_ref, own, shared):
        own[...] = dot_tn(k_ref[...], f_ref[:, :width])
        shared[...] = dot_tn(f_ref[:, width : 2 * width], f_ref[:, 2 * width :])

    return call(
        body,
        [shape(width, width, dtype=f32), shape(width, half, dtype=f32)],
        [VMEM] * 2,
        [],
        16,
        3 * keys.shape[0] * width * width,
        9 * width * width,
        "keep",
    )(keys, factors)


def chip_sum(own_keep, own_got, shared_keep, shared_got):
    width, half = shared_keep.shape
    rows = width // NY
    wide = width + half

    def body(ok_ref, og_ref, sk_ref, sg_ref, mine, *outs):
        for step in range(NY):
            start = lax.rem(own_y() + step, NY) * rows
            for part in range(2):
                cut = rows // 2
                span = pl.ds(pl.multiple_of(start + part * cut, cut), cut)
                own = ok_ref[span, :] + og_ref[span, :].astype(f32)
                shared = sk_ref[span, :] + sg_ref[span, :].astype(f32)
                if step == 0:
                    mine[part * cut : (part + 1) * cut, :width] = own
                    mine[part * cut : (part + 1) * cut, width:] = shared
                else:
                    out = outs[2 * (step - 1) + part]
                    out[:, :width] = own.astype(bf16)
                    out[:, width:] = shared.astype(bf16)

    return call(
        body,
        [shape(rows, wide, dtype=f32)] + [shape(rows // 2, wide)] * (2 * NY - 2),
        [VMEM] * 4,
        [],
        16,
        0,
        10 * width * wide,
        "chip_sum",
    )(own_keep, own_got, shared_keep, shared_got)


def assemble(own, previous, following, opposite):
    rows, wide = own.shape
    width = rows * NY
    pieces = [own, *following, *opposite, *previous]

    def body(own_ref, *rest):
        parts, (x_ref, s_ref) = rest[:-2], rest[-2:]
        base = own_y()
        start = pl.multiple_of(base * rows, rows)
        x_ref[pl.ds(start, rows), :] = own_ref[:, :width]
        s_ref[pl.ds(start, rows), :] = own_ref[:, width:]
        for n, part in enumerate(parts):
            cut = rows // 2
            start = lax.rem(base + 1 + n // 2, NY) * rows + (n % 2) * cut
            span = pl.ds(pl.multiple_of(start, cut), cut)
            x_ref[span, :] = part[:, :width]
            s_ref[span, :] = part[:, width:]

    return call(
        body,
        [shape(width, width), shape(width, wide - width)],
        [VMEM] * len(pieces),
        [],
        16,
        0,
        4 * width * wide,
        "assemble",
    )(*pieces)


def newton_schulz(x_ref, w_ref, w_copy, outs, gram, poly, other):
    width = x_ref.shape[0]
    blocks = [slice(row, row + ROWS) for row in range(0, width, ROWS)]

    def store(ref, n, below):
        rows = blocks[n]
        ref[rows, : rows.stop] = below
        for column in blocks[:n]:
            ref[column, rows] = below[:, column].T

    square_sum = jnp.zeros((1, 1), f32)
    for rows in blocks:
        wide = x_ref[rows, :].astype(f32)
        square_sum = square_sum + jnp.sum(wide * wide).reshape(1, 1)
    scale = 1.0 / (jnp.sqrt(square_sum) + eps)
    now = x_ref
    for turn in range(NS_ITERS):
        for n, rows in enumerate(blocks):
            product = dot_nt(now[rows, :], now[: rows.stop, :])
            if turn == 0:
                product = product * (scale * scale)
            store(gram, n, product.astype(bf16))
        for n, rows in enumerate(blocks):
            squared = dot(gram[rows, :], gram[:, : rows.stop])
            linear = gram[rows, : rows.stop].astype(f32)
            store(poly, n, (ns_b * linear + ns_c * squared).astype(bf16))
        if turn == NS_ITERS - 1:
            w_copy.wait()
        for rows in blocks:
            new = ns_a * now[rows, :].astype(f32) + dot(poly[rows, :], now[...])
            if turn == 0:
                new = new * scale
            new = new.astype(bf16)
            if turn < NS_ITERS - 1:
                other[rows, :] = new
            else:
                step = step_scale * new.astype(f32)
                fresh = (w_ref[rows, :].astype(f32) - step).astype(bf16)
                for n, out in enumerate(outs):
                    height = out.shape[0]
                    start, stop = max(rows.start, n * height), min(rows.stop, (n + 1) * height)
                    if start < stop:
                        inside = slice(start - n * height, stop - n * height)
                        out[inside, :] = fresh[start - rows.start : stop - rows.start]
        now = other


def own_step(summed, weights):
    width = weights.shape[-1]

    def body(x_ref, w_hbm, top, bottom, gram, poly, other, w_ref, sem):
        copy = pltpu.make_async_copy(w_hbm.at[0, own_core()], w_ref, sem)
        copy.start()
        newton_schulz(x_ref, w_ref, copy, (top, bottom), gram, poly, other)

    return call(
        body,
        [shape(width // 2, width)] * 2,
        [VMEM, HBM],
        [pltpu.VMEM((width, width), bf16)] * 4 + [pltpu.SemaphoreType.DMA],
        20,
        10 * width**3,
        6 * width * width,
        "own_step",
    )(summed, weights)


def shared_step(mine, partners, weights):
    width = weights.shape[-1]
    half = width // 2

    def body(a_ref, b_ref, w_hbm, out_ref, gram, poly, other, x_ref, w_ref, sem):
        copy = pltpu.make_async_copy(w_hbm.at[0, 2], w_ref, sem)
        copy.start()
        first = own_core() == 0
        x_ref[:, :half] = jnp.where(first, a_ref[...], b_ref[...])
        x_ref[:, half:] = jnp.where(first, b_ref[...], a_ref[...])
        newton_schulz(x_ref, w_ref, copy, (out_ref,), gram, poly, other)

    return call(
        body,
        shape(width, width),
        [VMEM, VMEM, HBM],
        [pltpu.VMEM((width, width), bf16)] * 5 + [pltpu.SemaphoreType.DMA],
        20,
        10 * width**3,
        6 * width * width,
        "shared_step",
    )(mine, partners, weights)


def project(queries, own, other, shared, out_proj):
    tokens, width = queries.shape
    heads = out_proj.shape[1] // width

    half = width // 2

    def body(q_ref, own_a, own_b, other_a, other_b, shared_ref, p_ref, *outs):
        first = own_core() == 0
        left, right = q_ref[:, :half], q_ref[:, half:]
        q_own = dot(left, own_a[...]) + dot(right, own_b[...])
        q_other = dot(left, other_a[...]) + dot(right, other_b[...])
        q1 = jnp.where(first, q_own, q_other)
        q3 = jnp.where(first, q_other, q_own)
        gated = (q1 * jax.nn.sigmoid(q1) * q3).astype(bf16)
        outputs = dot(gated, shared_ref[...]).astype(bf16)
        cut = tokens // 2
        for step in range(heads):
            head = lax.rem(lax.axis_index("head") + step, heads)
            start = pl.multiple_of(head * width, width)
            product = dot(outputs, p_ref[:, pl.ds(start, width)])
            if step == 0:
                outs[0][...] = product
            else:
                outs[2 * step - 1][...] = product[:cut].astype(bf16)
                outs[2 * step][...] = product[cut:].astype(bf16)

    return call(
        body,
        [shape(tokens, width, dtype=f32)] + [shape(tokens // 2, width)] * (2 * heads - 2),
        [VMEM] * 7,
        [],
        20,
        2 * tokens * width * width * (3 + heads),
        16 * width * width,
        "project",
    )(queries, *own, *other, shared, out_proj)


def mix(own, sum_a, sum_b, direct_a, direct_b):
    tokens, width = own.shape
    cut = tokens // 2

    def body(sum_a_ref, sum_b_ref, direct_a_ref, direct_b_ref, own_ref, out):
        halves = [(sum_a_ref, direct_a_ref), (sum_b_ref, direct_b_ref)]
        for part, (relayed, direct) in enumerate(halves):
            span = slice(part * cut, (part + 1) * cut)
            total = own_ref[span, :] + relayed[...].astype(f32) + direct[...].astype(f32)
            out[:, span] = total.T.astype(bf16)

    return call(
        body, shape(width, tokens), [VMEM] * 5, [], 16, 0, 12 * tokens * width, "mix"
    )(sum_a, sum_b, direct_a, direct_b, own)


def shift(array, axis, pairs):
    return lax.ppermute(array, axis, pairs)


def add(left, right):
    return (left.astype(f32) + right.astype(f32)).astype(bf16)


def ring_sum(pieces, axis, up, down):
    next_a, next_b, far_a, far_b, previous_a, previous_b = pieces
    relay_a = shift(far_a, axis, up)
    relay_b = shift(far_b, axis, down)
    from_down_b = shift(next_b, axis, up)
    from_up_a = shift(previous_a, axis, down)
    from_down_a = shift(add(next_a, relay_a), axis, up)
    from_up_b = shift(add(previous_b, relay_b), axis, down)
    return from_down_a, from_up_b, from_up_a, from_down_b


def ring_gather(block, axis, up, down):
    cut = block.shape[0] // 2
    block_a, block_b = block[:cut], block[cut:]
    previous_a = shift(block_a, axis, up)
    following_b = shift(block_b, axis, down)
    previous_b = shift(block_b, axis, up)
    following_a = shift(block_a, axis, down)
    far_a = shift(previous_a, axis, up)
    far_b = shift(following_b, axis, down)
    return (previous_a, previous_b), (following_a, following_b), (far_a, far_b)


def on_device(keys, values, rates, fast_weights, queries, out_proj):
    width = fast_weights.shape[-1]
    heads = lax.axis_size("head")

    own_send, shared_send, factors = gradients(
        keys, values, rates.reshape(-1, 128), fast_weights
    )
    own_got = swap_cores(own_send)
    shared_got = swap_cores(shared_send)
    own_keep, shared_keep = keep(keys, factors)
    mine, *shares = chip_sum(own_keep, own_got, shared_keep, shared_got)

    sum_a, sum_b, direct_a, direct_b = ring_sum(shares, "tok", Y_UP, Y_DOWN)
    relayed = jnp.concatenate([sum_a, sum_b]).astype(f32)
    direct = jnp.concatenate([direct_a, direct_b]).astype(f32)
    y_sum = (relayed + direct + mine).astype(bf16)
    z_sum = sum_shares(y_sum.reshape(NZ, width // NY // NZ, -1), Z_GROUPS)
    y_rows = gather_rows(z_sum, Z_GROUPS)
    previous, following, far = ring_gather(y_rows, "tok", Y_UP, Y_DOWN)
    own_sum, shared_part = assemble(y_rows, previous, following, far)

    shared_other = swap_cores(shared_part)
    own_fresh = own_step(own_sum, fast_weights)
    other_fresh = [swap_cores(rows) for rows in own_fresh]
    shared_fresh = shared_step(shared_part, shared_other, fast_weights)

    mixed, *shares = project(queries, own_fresh, other_fresh, shared_fresh, out_proj)
    up = [(i, (i + 1) % heads) for i in range(heads)]
    down = [(i, (i - 1) % heads) for i in range(heads)]
    return mix(mixed, *ring_sum(shares, "head", up, down))


def solution(mesh):
    in_specs = (
        P("tok", "head"),
        P("tok", "head"),
        P("tok", "head"),
        P("head", None, None, None),
        P("tok", "head"),
        P("head", None),
    )
    out_specs = P("head", "tok")
    return jax.shard_map(
        on_device, mesh=mesh, in_specs=in_specs, out_specs=out_specs, check_vma=False
    )
```

```python
import jax
import jax.numpy as jnp
from jax import lax
from jax.experimental import pallas as pl
from jax.experimental.pallas import tpu as pltpu
from jax.sharding import PartitionSpec as P

NS_ITERS = 2


ns_a = 3.4445
ns_b = -4.775
ns_c = 2.0315
step_scale = 1.0
eps = 1e-07

f32 = jnp.float32
bf16 = jnp.bfloat16

NY, NZ, NC = 4, 8, 2
ROWS = 256


def chip_index(y, z, core):
    return (y * NZ + z) * NC + core


Z_GROUPS = [
    [chip_index(y, z, core) for z in range(NZ)] for y in range(NY) for core in range(NC)
]
Y_UP = [(d, (d + NZ * NC) % (NY * NZ * NC)) for d in range(NY * NZ * NC)]
Y_DOWN = [(there, here) for here, there in Y_UP]
CORE_SWAP = [(device, device ^ 1) for device in range(NY * NZ * NC)]

VMEM = pl.BlockSpec(memory_space=pltpu.VMEM)
HBM = pl.BlockSpec(memory_space=pltpu.HBM)


def swap_cores(array):
    return lax.ppermute(array, "tok", CORE_SWAP)


def exchange(blocks, groups):
    return lax.all_to_all(blocks, "tok", 0, 0, axis_index_groups=groups)


def sum_shares(blocks, groups):
    return jnp.sum(exchange(blocks, groups).astype(f32), axis=0).astype(bf16)


def gather_rows(rows, groups):
    size = len(groups[0])
    gathered = exchange(jnp.broadcast_to(rows[None], (size,) + rows.shape), groups)
    return gathered.reshape(-1, rows.shape[1])


def dot(left, right):
    return jnp.dot(left, right, preferred_element_type=f32)


def dot_nt(left, right):
    return lax.dot_general(left, right, (((1,), (1,)), ((), ())), preferred_element_type=f32)


def dot_tn(left, right):
    return lax.dot_general(left, right, (((0,), (0,)), ((), ())), preferred_element_type=f32)


def sigmoid(x):
    return 0.5 + 0.5 * jnp.tanh(0.5 * x)


def call(body, outs, in_specs, scratch, mib, flops, moved, name, out_specs=None):
    if out_specs is None:
        out_specs = [VMEM] * len(outs) if isinstance(outs, list) else VMEM
    return pl.pallas_call(
        body,
        out_shape=outs,
        in_specs=in_specs,
        out_specs=out_specs,
        scratch_shapes=scratch,
        compiler_params=pltpu.CompilerParams(vmem_limit_bytes=mib << 20),
        cost_estimate=pl.CostEstimate(flops=flops, bytes_accessed=moved, transcendentals=0),
        name=name,
    )


def own_core():
    return lax.rem(lax.axis_index("tok"), NC)


def own_y():
    return lax.div(lax.axis_index("tok"), NZ * NC)


def shape(*dims, dtype=bf16):
    return jax.ShapeDtypeStruct(dims, dtype)


def gradients(keys, values, rates, weights):
    tokens, width = keys.shape
    half = width // 2
    lanes = rates.shape[1]
    parts = tokens // ROWS

    def body(r_ref, k_hbm, v_hbm, w_hbm, own_out, shared_out, factors_out,
             k_ref, v_ref, w_ref, errors, hidden, grads, own_send, shared_send, sems, out_sems):
        moves = [
            (k_hbm, k_ref),
            (w_hbm.at[0, 0], w_ref.at[0]),
            (w_hbm.at[0, 1], w_ref.at[1]),
            (v_hbm, v_ref),
            (w_hbm.at[0, 2], w_ref.at[2]),
        ]
        copies = [
            pltpu.make_async_copy(src, dst, sems.at[n]) for n, (src, dst) in enumerate(moves)
        ]
        for copy in copies:
            copy.start()
        stores = []

        def store(src, dst):
            copy = pltpu.make_async_copy(src, dst, out_sems.at[len(stores)])
            copy.start()
            stores.append(copy)

        core = own_core()
        kept = pl.ds(pl.multiple_of(core * half, half), half)
        sent = pl.ds(pl.multiple_of((1 - core) * half, half), half)
        rate_columns = r_ref[...].T
        copies[0].wait()
        copies[1].wait()
        for row in range(0, tokens, ROWS):
            rows = slice(row, row + ROWS)
            k = k_ref[rows, :]
            h1 = dot(k, w_ref[0])
            if row == 0:
                copies[2].wait()
            h3 = dot(k, w_ref[1])
            sig = sigmoid(h1)
            act = h1 * sig
            hidden[rows, :] = (act * h3).astype(bf16)
            store(hidden.at[rows, :], factors_out.at[rows, width : 2 * width])
            if row == 0:
                copies[3].wait()
            for part in range(row, row + ROWS, lanes):
                rate = rate_columns[:, part // lanes : part // lanes + 1]
                span = slice(part, part + lanes)
                errors[span, :] = (-rate * v_ref[span, :].astype(f32)).astype(bf16)
            store(errors.at[rows, kept], factors_out.at[rows, 2 * width :])
            if row == 0:
                copies[4].wait()
            dz = dot_nt(errors[rows, :], w_ref[2])
            slope = sig + act * (1.0 - sig)
            grads[core, rows, :] = (dz * h3 * slope).astype(bf16)
            grads[1 - core, rows, :] = (dz * act).astype(bf16)
            store(grads.at[0, rows, :], factors_out.at[rows, :width])
        own_send[...] = dot_tn(k_ref[...], grads[1]).astype(bf16)
        store(own_send, own_out)
        shared_send[...] = dot_tn(hidden[...], errors[:, sent]).astype(bf16)
        store(shared_send, shared_out)
        for copy in stores:
            copy.wait()

    results = [(width, width), (width, half), (tokens, 2 * width + half)]
    wide = pltpu.VMEM((tokens, width), bf16)
    return call(
        body,
        [shape(*dims) for dims in results],
        [VMEM] + [HBM] * 3,
        [wide, wide, pltpu.VMEM((3, width, width), bf16), wide, wide]
        + [pltpu.VMEM((2, tokens, width), bf16)]
        + [pltpu.VMEM(dims, bf16) for dims in results[:2]]
        + [pltpu.SemaphoreType.DMA((5,)), pltpu.SemaphoreType.DMA((3 * parts + 2,))],
        60,
        9 * tokens * width * width,
        12 * width * width,
        "gradients",
        [HBM] * len(results),
    )(rates, keys, values, weights)


def keep(keys, factors):
    width = keys.shape[1]
    half = width // 2

    def body(k_ref, f_ref, own, shared):
        own[...] = dot_tn(k_ref[...], f_ref[:, :width])
        shared[...] = dot_tn(f_ref[:, width : 2 * width], f_ref[:, 2 * width :])

    return call(
        body,
        [shape(width, width, dtype=f32), shape(width, half, dtype=f32)],
        [VMEM] * 2,
        [],
        16,
        3 * keys.shape[0] * width * width,
        9 * width * width,
        "keep",
    )(keys, factors)


def chip_sum(own_keep, own_got, shared_keep, shared_got):
    width, half = shared_keep.shape
    rows = width // NY
    wide = width + half

    def body(ok_ref, og_ref, sk_ref, sg_ref, mine, *outs):
        for step in range(NY):
            start = lax.rem(own_y() + step, NY) * rows
            for part in range(2):
                cut = rows // 2
                span = pl.ds(pl.multiple_of(start + part * cut, cut), cut)
                own = ok_ref[span, :] + og_ref[span, :].astype(f32)
                shared = sk_ref[span, :] + sg_ref[span, :].astype(f32)
                if step == 0:
                    mine[part * cut : (part + 1) * cut, :width] = own
                    mine[part * cut : (part + 1) * cut, width:] = shared
                else:
                    out = outs[2 * (step - 1) + part]
                    out[:, :width] = own.astype(bf16)
                    out[:, width:] = shared.astype(bf16)

    return call(
        body,
        [shape(rows, wide, dtype=f32)] + [shape(rows // 2, wide)] * (2 * NY - 2),
        [VMEM] * 4,
        [],
        16,
        0,
        10 * width * wide,
        "chip_sum",
    )(own_keep, own_got, shared_keep, shared_got)


def assemble(own, previous, following, opposite):
    rows, wide = own.shape
    width = rows * NY
    pieces = [own, *following, *opposite, *previous]

    def body(own_ref, *rest):
        parts, (x_ref, s_ref) = rest[:-2], rest[-2:]
        base = own_y()
        start = pl.multiple_of(base * rows, rows)
        x_ref[pl.ds(start, rows), :] = own_ref[:, :width]
        s_ref[pl.ds(start, rows), :] = own_ref[:, width:]
        for n, part in enumerate(parts):
            cut = rows // 2
            start = lax.rem(base + 1 + n // 2, NY) * rows + (n % 2) * cut
            span = pl.ds(pl.multiple_of(start, cut), cut)
            x_ref[span, :] = part[:, :width]
            s_ref[span, :] = part[:, width:]

    return call(
        body,
        [shape(width, width), shape(width, wide - width)],
        [VMEM] * len(pieces),
        [],
        16,
        0,
        4 * width * wide,
        "assemble",
    )(*pieces)


def newton_schulz(x_ref, w_ref, outs, gram, poly, other):
    width = x_ref.shape[0]
    blocks = [slice(row, row + ROWS) for row in range(0, width, ROWS)]

    def store(ref, n, below):
        rows = blocks[n]
        ref[rows, : rows.stop] = below
        for column in blocks[:n]:
            ref[column, rows] = below[:, column].T

    square_sum = jnp.zeros((1, 1), f32)
    for rows in blocks:
        wide = x_ref[rows, :].astype(f32)
        square_sum = square_sum + jnp.sum(wide * wide).reshape(1, 1)
    scale = 1.0 / (jnp.sqrt(square_sum) + eps)
    now = x_ref
    for turn in range(NS_ITERS):
        for n, rows in enumerate(blocks):
            product = dot_nt(now[rows, :], now[: rows.stop, :])
            if turn == 0:
                product = product * (scale * scale)
            store(gram, n, product.astype(bf16))
        for n, rows in enumerate(blocks):
            squared = dot(gram[rows, :], gram[:, : rows.stop])
            linear = gram[rows, : rows.stop].astype(f32)
            store(poly, n, (ns_b * linear + ns_c * squared).astype(bf16))
        for rows in blocks:
            new = ns_a * now[rows, :].astype(f32) + dot(poly[rows, :], now[...])
            if turn == 0:
                new = new * scale
            new = new.astype(bf16)
            if turn < NS_ITERS - 1:
                other[rows, :] = new
            else:
                step = step_scale * new.astype(f32)
                fresh = (w_ref[rows, :].astype(f32) - step).astype(bf16)
                for n, out in enumerate(outs):
                    height = out.shape[0]
                    start, stop = max(rows.start, n * height), min(rows.stop, (n + 1) * height)
                    if start < stop:
                        inside = slice(start - n * height, stop - n * height)
                        out[inside, :] = fresh[start - rows.start : stop - rows.start]
        now = other


def own_step(summed, weights):
    width = weights.shape[-1]

    def body(x_ref, w_ref, top, bottom, gram, poly, other):
        newton_schulz(x_ref, w_ref.at[0, own_core()], (top, bottom), gram, poly, other)

    return call(
        body,
        [shape(width // 2, width)] * 2,
        [VMEM] * 2,
        [pltpu.VMEM((width, width), bf16)] * 3,
        16,
        10 * width**3,
        6 * width * width,
        "own_step",
    )(summed, weights)


def shared_step(mine, partners, weights):
    width = weights.shape[-1]
    half = width // 2

    def body(a_ref, b_ref, w_ref, out_ref, gram, poly, other, x_ref):
        first = own_core() == 0
        x_ref[:, :half] = jnp.where(first, a_ref[...], b_ref[...])
        x_ref[:, half:] = jnp.where(first, b_ref[...], a_ref[...])
        newton_schulz(x_ref, w_ref.at[0, 2], (out_ref,), gram, poly, other)

    return call(
        body,
        shape(width, width),
        [VMEM] * 3,
        [pltpu.VMEM((width, width), bf16)] * 4,
        16,
        10 * width**3,
        6 * width * width,
        "shared_step",
    )(mine, partners, weights)


def project(queries, own, other, shared, out_proj):
    tokens, width = queries.shape
    heads = out_proj.shape[1] // width

    half = width // 2

    def body(q_ref, own_a, own_b, other_a, other_b, shared_ref, p_ref, *outs):
        first = own_core() == 0
        left, right = q_ref[:, :half], q_ref[:, half:]
        q_own = dot(left, own_a[...]) + dot(right, own_b[...])
        q_other = dot(left, other_a[...]) + dot(right, other_b[...])
        q1 = jnp.where(first, q_own, q_other)
        q3 = jnp.where(first, q_other, q_own)
        gated = (q1 * sigmoid(q1) * q3).astype(bf16)
        outputs = dot(gated, shared_ref[...]).astype(bf16)
        cut = tokens // 2
        for step in range(heads):
            head = lax.rem(lax.axis_index("head") + step, heads)
            start = pl.multiple_of(head * width, width)
            product = dot(outputs, p_ref[:, pl.ds(start, width)])
            if step == 0:
                outs[0][...] = product
            else:
                outs[2 * step - 1][...] = product[:cut].astype(bf16)
                outs[2 * step][...] = product[cut:].astype(bf16)

    return call(
        body,
        [shape(tokens, width, dtype=f32)] + [shape(tokens // 2, width)] * (2 * heads - 2),
        [VMEM] * 7,
        [],
        20,
        2 * tokens * width * width * (3 + heads),
        16 * width * width,
        "project",
    )(queries, *own, *other, shared, out_proj)


def mix(own, sum_a, sum_b, direct_a, direct_b):
    tokens, width = own.shape
    cut = tokens // 2

    def body(sum_a_ref, sum_b_ref, direct_a_ref, direct_b_ref, own_ref, out):
        halves = [(sum_a_ref, direct_a_ref), (sum_b_ref, direct_b_ref)]
        for part, (relayed, direct) in enumerate(halves):
            span = slice(part * cut, (part + 1) * cut)
            total = own_ref[span, :] + relayed[...].astype(f32) + direct[...].astype(f32)
            out[:, span] = total.T.astype(bf16)

    return call(
        body, shape(width, tokens), [VMEM] * 5, [], 16, 0, 12 * tokens * width, "mix"
    )(sum_a, sum_b, direct_a, direct_b, own)


def shift(array, axis, pairs):
    return lax.ppermute(array, axis, pairs)


def add(left, right):
    return (left.astype(f32) + right.astype(f32)).astype(bf16)


def ring_sum(pieces, axis, up, down):
    next_a, next_b, far_a, far_b, previous_a, previous_b = pieces
    relay_a = shift(far_a, axis, up)
    relay_b = shift(far_b, axis, down)
    from_down_b = shift(next_b, axis, up)
    from_up_a = shift(previous_a, axis, down)
    from_down_a = shift(add(next_a, relay_a), axis, up)
    from_up_b = shift(add(previous_b, relay_b), axis, down)
    return from_down_a, from_up_b, from_up_a, from_down_b


def ring_gather(block, axis, up, down):
    cut = block.shape[0] // 2
    block_a, block_b = block[:cut], block[cut:]
    previous_a = shift(block_a, axis, up)
    following_b = shift(block_b, axis, down)
    previous_b = shift(block_b, axis, up)
    following_a = shift(block_a, axis, down)
    far_a = shift(previous_a, axis, up)
    far_b = shift(following_b, axis, down)
    return (previous_a, previous_b), (following_a, following_b), (far_a, far_b)


def on_device(keys, values, rates, fast_weights, queries, out_proj):
    width = fast_weights.shape[-1]
    heads = lax.axis_size("head")

    own_send, shared_send, factors = gradients(
        keys, values, rates.reshape(-1, 128), fast_weights
    )
    own_got = swap_cores(own_send)
    shared_got = swap_cores(shared_send)
    own_keep, shared_keep = keep(keys, factors)
    mine, *shares = chip_sum(own_keep, own_got, shared_keep, shared_got)

    sum_a, sum_b, direct_a, direct_b = ring_sum(shares, "tok", Y_UP, Y_DOWN)
    relayed = jnp.concatenate([sum_a, sum_b]).astype(f32)
    direct = jnp.concatenate([direct_a, direct_b]).astype(f32)
    y_sum = (relayed + direct + mine).astype(bf16)
    z_sum = sum_shares(y_sum.reshape(NZ, width // NY // NZ, -1), Z_GROUPS)
    y_rows = gather_rows(z_sum, Z_GROUPS)
    previous, following, far = ring_gather(y_rows, "tok", Y_UP, Y_DOWN)
    own_sum, shared_part = assemble(y_rows, previous, following, far)

    shared_other = swap_cores(shared_part)
    own_fresh = own_step(own_sum, fast_weights)
    other_fresh = [swap_cores(rows) for rows in own_fresh]
    shared_fresh = shared_step(shared_part, shared_other, fast_weights)

    mixed, *shares = project(queries, own_fresh, other_fresh, shared_fresh, out_proj)
    up = [(i, (i + 1) % heads) for i in range(heads)]
    down = [(i, (i - 1) % heads) for i in range(heads)]
    return mix(mixed, *ring_sum(shares, "head", up, down))


def solution(mesh):
    in_specs = (
        P("tok", "head"),
        P("tok", "head"),
        P("tok", "head"),
        P("head", None, None, None),
        P("tok", "head"),
        P("head", None),
    )
    out_specs = P("head", "tok")
    return jax.shard_map(
        on_device, mesh=mesh, in_specs=in_specs, out_specs=out_specs, check_vma=False
    )
```

```python
import jax
import jax.numpy as jnp
from jax import lax
from jax.experimental import pallas as pl
from jax.experimental.pallas import tpu as pltpu
from jax.sharding import PartitionSpec as P

NS_ITERS = 2


ns_a = 3.4445
ns_b = -4.775
ns_c = 2.0315
step_scale = 1.0
eps = 1e-07

f32 = jnp.float32
bf16 = jnp.bfloat16

NY, NZ, NC = 4, 8, 2
ROWS = 256


def chip_index(y, z, core):
    return (y * NZ + z) * NC + core


Z_GROUPS = [
    [chip_index(y, z, core) for parity in range(2) for z in range(parity, NZ, 2)]
    for y in range(NY)
    for core in range(NC)
]
PARITY_GROUPS = [
    [chip_index(y, z, core) for z in range(parity, NZ, 2)]
    for y in range(NY)
    for parity in range(2)
    for core in range(NC)
]


def moved(up, flip):
    return [
        (chip_index(y, z, core), chip_index((y + up) % NY, z ^ flip, core))
        for y in range(NY)
        for z in range(NZ)
        for core in range(NC)
    ]


CORE_SWAP = [(device, device ^ 1) for device in range(NY * NZ * NC)]

VMEM = pl.BlockSpec(memory_space=pltpu.VMEM)
HBM = pl.BlockSpec(memory_space=pltpu.HBM)


def swap_cores(array):
    return lax.ppermute(array, "tok", CORE_SWAP)


def exchange(blocks, groups):
    return lax.all_to_all(blocks, "tok", 0, 0, axis_index_groups=groups)


def dot(left, right):
    return jnp.dot(left, right, preferred_element_type=f32)


def dot_nt(left, right):
    return lax.dot_general(left, right, (((1,), (1,)), ((), ())), preferred_element_type=f32)


def dot_tn(left, right):
    return lax.dot_general(left, right, (((0,), (0,)), ((), ())), preferred_element_type=f32)


def sigmoid(x):
    return 0.5 + 0.5 * jnp.tanh(0.5 * x)


def call(body, outs, in_specs, scratch, mib, flops, moved, name, out_specs=None):
    if out_specs is None:
        out_specs = [VMEM] * len(outs) if isinstance(outs, list) else VMEM
    return pl.pallas_call(
        body,
        out_shape=outs,
        in_specs=in_specs,
        out_specs=out_specs,
        scratch_shapes=scratch,
        compiler_params=pltpu.CompilerParams(vmem_limit_bytes=mib << 20),
        cost_estimate=pl.CostEstimate(flops=flops, bytes_accessed=moved, transcendentals=0),
        name=name,
    )


def own_core():
    return lax.rem(lax.axis_index("tok"), NC)


def own_parity():
    return lax.rem(lax.div(lax.axis_index("tok"), NC), 2)


def own_y():
    return lax.div(lax.axis_index("tok"), NZ * NC)


def shape(*dims, dtype=bf16):
    return jax.ShapeDtypeStruct(dims, dtype)


def gradients(keys, values, rates, weights):
    tokens, width = keys.shape
    half = width // 2
    lanes = rates.shape[1]
    parts = tokens // ROWS

    def body(r_ref, k_hbm, v_hbm, w_hbm, own_out, shared_out, factors_out,
             k_ref, v_ref, w_ref, errors, hidden, grads, own_send, shared_send, sems, out_sems):
        moves = [
            (k_hbm, k_ref),
            (w_hbm.at[0, 0], w_ref.at[0]),
            (w_hbm.at[0, 1], w_ref.at[1]),
            (v_hbm, v_ref),
            (w_hbm.at[0, 2], w_ref.at[2]),
        ]
        copies = [
            pltpu.make_async_copy(src, dst, sems.at[n]) for n, (src, dst) in enumerate(moves)
        ]
        for copy in copies:
            copy.start()
        stores = []

        def store(src, dst):
            copy = pltpu.make_async_copy(src, dst, out_sems.at[len(stores)])
            copy.start()
            stores.append(copy)

        core = own_core()
        kept = pl.ds(pl.multiple_of(core * half, half), half)
        sent = pl.ds(pl.multiple_of((1 - core) * half, half), half)
        rate_columns = r_ref[...].T
        copies[0].wait()
        copies[1].wait()
        for row in range(0, tokens, ROWS):
            rows = slice(row, row + ROWS)
            k = k_ref[rows, :]
            h1 = dot(k, w_ref[0])
            if row == 0:
                copies[2].wait()
            h3 = dot(k, w_ref[1])
            sig = sigmoid(h1)
            act = h1 * sig
            hidden[rows, :] = (act * h3).astype(bf16)
            store(hidden.at[rows, :], factors_out.at[rows, width : 2 * width])
            if row == 0:
                copies[3].wait()
            for part in range(row, row + ROWS, lanes):
                rate = rate_columns[:, part // lanes : part // lanes + 1]
                span = slice(part, part + lanes)
                errors[span, :] = (-rate * v_ref[span, :].astype(f32)).astype(bf16)
            store(errors.at[rows, kept], factors_out.at[rows, 2 * width :])
            if row == 0:
                copies[4].wait()
            dz = dot_nt(errors[rows, :], w_ref[2])
            slope = sig + act * (1.0 - sig)
            grads[core, rows, :] = (dz * h3 * slope).astype(bf16)
            grads[1 - core, rows, :] = (dz * act).astype(bf16)
            store(grads.at[0, rows, :], factors_out.at[rows, :width])
        shared_send[...] = dot_tn(hidden[...], errors[:, sent]).astype(bf16)
        store(shared_send, shared_out)
        for row in range(0, width, ROWS):
            rows = slice(row, row + ROWS)
            own_send[rows, :] = dot_tn(k_ref[:, rows], grads[1]).astype(bf16)
            store(own_send.at[rows, :], own_out.at[rows, :])
        for copy in stores:
            copy.wait()

    results = [(width, width), (width, half), (tokens, 2 * width + half)]
    wide = pltpu.VMEM((tokens, width), bf16)
    return call(
        body,
        [shape(*dims) for dims in results],
        [VMEM] + [HBM] * 3,
        [wide, wide, pltpu.VMEM((3, width, width), bf16), wide, wide]
        + [pltpu.VMEM((2, tokens, width), bf16)]
        + [pltpu.VMEM(dims, bf16) for dims in results[:2]]
        + [pltpu.SemaphoreType.DMA((5,)), pltpu.SemaphoreType.DMA((3 * parts + 1 + width // ROWS,))],
        60,
        9 * tokens * width * width,
        12 * width * width,
        "gradients",
        [HBM] * len(results),
    )(rates, keys, values, weights)


def keep(keys, factors):
    width = keys.shape[1]
    half = width // 2

    def body(k_ref, f_ref, own, shared):
        own[...] = dot_tn(k_ref[...], f_ref[:, :width])
        shared[...] = dot_tn(f_ref[:, width : 2 * width], f_ref[:, 2 * width :])

    return call(
        body,
        [shape(width, width, dtype=f32), shape(width, half, dtype=f32)],
        [VMEM] * 2,
        [],
        16,
        3 * keys.shape[0] * width * width,
        9 * width * width,
        "keep",
    )(keys, factors)


def chip_sum(own_keep, own_got, shared_keep, shared_got):
    width, half = shared_keep.shape
    cut = width // NY // 2
    wide = width + half

    def body(ok_ref, og_ref, sk_ref, sg_ref, *outs):
        for n, out in enumerate(outs):
            block = lax.rem(own_y() + n // 2, NY) * 2
            side = own_parity() if n % 2 == 0 else 1 - own_parity()
            span = pl.ds(pl.multiple_of((block + side) * cut, cut), cut)
            own = ok_ref[span, :] + og_ref[span, :].astype(f32)
            shared = sk_ref[span, :] + sg_ref[span, :].astype(f32)
            out[:, :width] = own.astype(out.dtype)
            out[:, width:] = shared.astype(out.dtype)

    return call(
        body,
        [shape(cut, wide, dtype=f32)] + [shape(cut, wide)] * (2 * NY - 1),
        [VMEM] * 4,
        [],
        16,
        0,
        10 * width * wide,
        "chip_sum",
    )(own_keep, own_got, shared_keep, shared_got)


def assemble(own, previous, following, opposite):
    rows, wide = own.shape
    width = rows * NY
    pieces = [own, *following, *opposite, *previous]

    def body(own_ref, *rest):
        parts, (x_ref, s_ref) = rest[:-2], rest[-2:]
        base = own_y()
        start = pl.multiple_of(base * rows, rows)
        x_ref[pl.ds(start, rows), :] = own_ref[:, :width]
        s_ref[pl.ds(start, rows), :] = own_ref[:, width:]
        for n, part in enumerate(parts):
            cut = rows // 2
            start = lax.rem(base + 1 + n // 2, NY) * rows + (n % 2) * cut
            span = pl.ds(pl.multiple_of(start, cut), cut)
            x_ref[span, :] = part[:, :width]
            s_ref[span, :] = part[:, width:]

    return call(
        body,
        [shape(width, width), shape(width, wide - width)],
        [VMEM] * len(pieces),
        [],
        16,
        0,
        4 * width * wide,
        "assemble",
    )(*pieces)


def newton_schulz(x_ref, w_ref, outs, gram, poly, other):
    width = x_ref.shape[0]
    blocks = [slice(row, row + ROWS) for row in range(0, width, ROWS)]

    def store(ref, n, below):
        rows = blocks[n]
        ref[rows, : rows.stop] = below
        for column in blocks[:n]:
            ref[column, rows] = below[:, column].T

    square_sum = jnp.zeros((1, 1), f32)
    for rows in blocks:
        wide = x_ref[rows, :].astype(f32)
        square_sum = square_sum + jnp.sum(wide * wide).reshape(1, 1)
    scale = 1.0 / (jnp.sqrt(square_sum) + eps)
    now = x_ref
    for turn in range(NS_ITERS):
        for n, rows in enumerate(blocks):
            product = dot_nt(now[rows, :], now[: rows.stop, :])
            if turn == 0:
                product = product * (scale * scale)
            store(gram, n, product.astype(bf16))
        for n, rows in enumerate(blocks):
            squared = dot(gram[rows, :], gram[:, : rows.stop])
            linear = gram[rows, : rows.stop].astype(f32)
            store(poly, n, (ns_b * linear + ns_c * squared).astype(bf16))
        for rows in blocks:
            new = ns_a * now[rows, :].astype(f32) + dot(poly[rows, :], now[...])
            if turn == 0:
                new = new * scale
            new = new.astype(bf16)
            if turn < NS_ITERS - 1:
                other[rows, :] = new
            else:
                step = step_scale * new.astype(f32)
                fresh = (w_ref[rows, :].astype(f32) - step).astype(bf16)
                for n, out in enumerate(outs):
                    height = out.shape[0]
                    start, stop = max(rows.start, n * height), min(rows.stop, (n + 1) * height)
                    if start < stop:
                        inside = slice(start - n * height, stop - n * height)
                        out[inside, :] = fresh[start - rows.start : stop - rows.start]
        now = other


def own_step(summed, weights):
    width = weights.shape[-1]

    def body(x_ref, w_ref, top, bottom, gram, poly, other):
        newton_schulz(x_ref, w_ref.at[0, own_core()], (top, bottom), gram, poly, other)

    return call(
        body,
        [shape(width // 2, width)] * 2,
        [VMEM] * 2,
        [pltpu.VMEM((width, width), bf16)] * 3,
        16,
        10 * width**3,
        6 * width * width,
        "own_step",
    )(summed, weights)


def shared_step(mine, partners, weights):
    width = weights.shape[-1]
    half = width // 2

    def body(a_ref, b_ref, w_ref, out_ref, gram, poly, other, x_ref):
        first = own_core() == 0
        x_ref[:, :half] = jnp.where(first, a_ref[...], b_ref[...])
        x_ref[:, half:] = jnp.where(first, b_ref[...], a_ref[...])
        newton_schulz(x_ref, w_ref.at[0, 2], (out_ref,), gram, poly, other)

    return call(
        body,
        shape(width, width),
        [VMEM] * 3,
        [pltpu.VMEM((width, width), bf16)] * 4,
        16,
        10 * width**3,
        6 * width * width,
        "shared_step",
    )(mine, partners, weights)


def project(queries, own, other, shared, out_proj):
    tokens, width = queries.shape
    heads = out_proj.shape[1] // width

    half = width // 2

    def body(q_ref, own_a, own_b, other_a, other_b, shared_ref, p_ref, *outs):
        first = own_core() == 0
        left, right = q_ref[:, :half], q_ref[:, half:]
        q_own = dot(left, own_a[...]) + dot(right, own_b[...])
        q_other = dot(left, other_a[...]) + dot(right, other_b[...])
        q1 = jnp.where(first, q_own, q_other)
        q3 = jnp.where(first, q_other, q_own)
        gated = (q1 * sigmoid(q1) * q3).astype(bf16)
        outputs = dot(gated, shared_ref[...]).astype(bf16)
        cut = tokens // 2
        for step in range(heads):
            head = lax.rem(lax.axis_index("head") + step, heads)
            start = pl.multiple_of(head * width, width)
            product = dot(outputs, p_ref[:, pl.ds(start, width)])
            if step == 0:
                outs[0][...] = product
            else:
                outs[2 * step - 1][...] = product[:cut].astype(bf16)
                outs[2 * step][...] = product[cut:].astype(bf16)

    return call(
        body,
        [shape(tokens, width, dtype=f32)] + [shape(tokens // 2, width)] * (2 * heads - 2),
        [VMEM] * 7,
        [],
        20,
        2 * tokens * width * width * (3 + heads),
        16 * width * width,
        "project",
    )(queries, *own, *other, shared, out_proj)


def mix(own, sum_a, sum_b, direct_a, direct_b):
    tokens, width = own.shape
    cut = tokens // 2

    def body(sum_a_ref, sum_b_ref, direct_a_ref, direct_b_ref, own_ref, out):
        halves = [(sum_a_ref, direct_a_ref), (sum_b_ref, direct_b_ref)]
        for part, (relayed, direct) in enumerate(halves):
            span = slice(part * cut, (part + 1) * cut)
            total = own_ref[span, :] + relayed[...].astype(f32) + direct[...].astype(f32)
            out[:, span] = total.T.astype(bf16)

    return call(
        body, shape(width, tokens), [VMEM] * 5, [], 16, 0, 12 * tokens * width, "mix"
    )(sum_a, sum_b, direct_a, direct_b, own)


def shift(array, axis, pairs):
    return lax.ppermute(array, axis, pairs)


def add(left, right):
    return (left.astype(f32) + right.astype(f32)).astype(bf16)


def ring_sum(pieces, axis, up, down):
    next_a, next_b, far_a, far_b, previous_a, previous_b = pieces
    relay_a = shift(far_a, axis, up)
    relay_b = shift(far_b, axis, down)
    from_down_b = shift(next_b, axis, up)
    from_up_a = shift(previous_a, axis, down)
    from_down_a = shift(add(next_a, relay_a), axis, up)
    from_up_b = shift(add(previous_b, relay_b), axis, down)
    return from_down_a, from_up_b, from_up_a, from_down_b


def y_parity_sum(mine, mine_z, next_x, next_z, far_x, far_z, previous_x, previous_z):
    relay_x = shift(far_x, "tok", moved(1, 0))
    relay_z = shift(far_z, "tok", moved(-1, 0))
    sum_x = shift(add(next_x, relay_x), "tok", moved(1, 0))
    sum_z = shift(add(previous_z, relay_z), "tok", moved(-1, 1))
    direct_x = shift(previous_x, "tok", moved(-1, 0))
    beside = shift(mine_z, "tok", moved(0, 1))
    direct_z = shift(next_z, "tok", moved(1, 1))
    total = sum_x.astype(f32) + sum_z.astype(f32)
    total = total + direct_x.astype(f32) + beside.astype(f32)
    return (total + direct_z.astype(f32) + mine).astype(bf16)


def sum_and_spread(blocks, times):
    def body(in_ref, out_ref):
        total = in_ref[0].astype(f32)
        for n in range(1, blocks.shape[0]):
            total = total + in_ref[n].astype(f32)
        for n in range(times):
            out_ref[n] = total.astype(bf16)

    spread = shape(times, *blocks.shape[1:])
    return call(body, spread, [VMEM], [], 16, 0, 6 * blocks.size, "sum_and_spread")(blocks)


def ring_gather(block, axis, up, down):
    cut = block.shape[0] // 2
    block_a, block_b = block[:cut], block[cut:]
    previous_a = shift(block_a, axis, up)
    following_b = shift(block_b, axis, down)
    previous_b = shift(block_b, axis, up)
    following_a = shift(block_a, axis, down)
    far_a = shift(previous_a, axis, up)
    far_b = shift(following_b, axis, down)
    return (previous_a, previous_b), (following_a, following_b), (far_a, far_b)


def on_device(keys, values, rates, fast_weights, queries, out_proj):
    width = fast_weights.shape[-1]
    heads = lax.axis_size("head")

    own_send, shared_send, factors = gradients(
        keys, values, rates.reshape(-1, 128), fast_weights
    )
    own_got = swap_cores(own_send)
    shared_got = swap_cores(shared_send)
    own_keep, shared_keep = keep(keys, factors)
    shares = chip_sum(own_keep, own_got, shared_keep, shared_got)

    y_sum = y_parity_sum(*shares)
    shares = exchange(y_sum.reshape(NZ // 2, width // NY // NZ, -1), PARITY_GROUPS)
    rows = exchange(sum_and_spread(shares, NZ), Z_GROUPS).reshape(width // NY, -1)
    previous, following, far = ring_gather(rows, "tok", moved(1, 0), moved(-1, 0))
    own_sum, shared_part = assemble(rows, previous, following, far)

    shared_other = swap_cores(shared_part)
    own_fresh = own_step(own_sum, fast_weights)
    other_fresh = [swap_cores(rows) for rows in own_fresh]
    shared_fresh = shared_step(shared_part, shared_other, fast_weights)

    mixed, *shares = project(queries, own_fresh, other_fresh, shared_fresh, out_proj)
    up = [(i, (i + 1) % heads) for i in range(heads)]
    down = [(i, (i - 1) % heads) for i in range(heads)]
    return mix(mixed, *ring_sum(shares, "head", up, down))


def solution(mesh):
    in_specs = (
        P("tok", "head"),
        P("tok", "head"),
        P("tok", "head"),
        P("head", None, None, None),
        P("tok", "head"),
        P("head", None),
    )
    out_specs = P("head", "tok")
    return jax.shard_map(
        on_device, mesh=mesh, in_specs=in_specs, out_specs=out_specs, check_vma=False
    )
```

```python
import jax
import jax.numpy as jnp
from jax import lax
from jax.experimental import pallas as pl
from jax.experimental.pallas import tpu as pltpu
from jax.sharding import PartitionSpec as P

NS_ITERS = 2


ns_a = 3.4445
ns_b = -4.775
ns_c = 2.0315
step_scale = 1.0
eps = 1e-07

f32 = jnp.float32
bf16 = jnp.bfloat16

NY, NZ, NC = 4, 8, 2
ROWS = 256


def chip_index(y, z, core):
    return (y * NZ + z) * NC + core


Z_GROUPS = [
    [chip_index(y, z, core) for parity in range(2) for z in reversed(range(parity, NZ, 2))]
    for y in range(NY)
    for core in range(NC)
]
PARITY_GROUPS = [
    [chip_index(y, z, core) for z in reversed(range(parity, NZ, 2))]
    for y in range(NY)
    for parity in range(2)
    for core in range(NC)
]


def moved(up, flip):
    return [
        (chip_index(y, z, core), chip_index((y + up) % NY, z ^ flip, core))
        for y in range(NY)
        for z in range(NZ)
        for core in range(NC)
    ]


CORE_SWAP = [(device, device ^ 1) for device in range(NY * NZ * NC)]

VMEM = pl.BlockSpec(memory_space=pltpu.VMEM)
HBM = pl.BlockSpec(memory_space=pltpu.HBM)


def swap_cores(array):
    return lax.ppermute(array, "tok", CORE_SWAP)


def exchange(blocks, groups):
    return lax.all_to_all(blocks, "tok", 0, 0, axis_index_groups=groups)


def dot(left, right):
    return jnp.dot(left, right, preferred_element_type=f32)


def dot_nt(left, right):
    return lax.dot_general(left, right, (((1,), (1,)), ((), ())), preferred_element_type=f32)


def dot_tn(left, right):
    return lax.dot_general(left, right, (((0,), (0,)), ((), ())), preferred_element_type=f32)


def sigmoid(x):
    return 0.5 + 0.5 * jnp.tanh(0.5 * x)


def call(body, outs, in_specs, scratch, mib, flops, moved, name, out_specs=None):
    if out_specs is None:
        out_specs = [VMEM] * len(outs) if isinstance(outs, list) else VMEM
    return pl.pallas_call(
        body,
        out_shape=outs,
        in_specs=in_specs,
        out_specs=out_specs,
        scratch_shapes=scratch,
        compiler_params=pltpu.CompilerParams(vmem_limit_bytes=mib << 20),
        cost_estimate=pl.CostEstimate(flops=flops, bytes_accessed=moved, transcendentals=0),
        name=name,
    )


def own_core():
    return lax.rem(lax.axis_index("tok"), NC)


def own_parity():
    return lax.rem(lax.div(lax.axis_index("tok"), NC), 2)


def own_y():
    return lax.div(lax.axis_index("tok"), NZ * NC)


def shape(*dims, dtype=bf16):
    return jax.ShapeDtypeStruct(dims, dtype)


def gradients(keys, values, rates, weights):
    tokens, width = keys.shape
    half = width // 2
    lanes = rates.shape[1]
    parts = tokens // ROWS

    def body(r_ref, k_hbm, v_hbm, w_hbm, own_out, shared_out, factors_out,
             k_ref, v_ref, w_ref, errors, hidden, grads, own_send, shared_send, sems, out_sems):
        moves = [
            (k_hbm, k_ref),
            (w_hbm.at[0, 0], w_ref.at[0]),
            (w_hbm.at[0, 1], w_ref.at[1]),
            (v_hbm, v_ref),
            (w_hbm.at[0, 2], w_ref.at[2]),
        ]
        copies = [
            pltpu.make_async_copy(src, dst, sems.at[n]) for n, (src, dst) in enumerate(moves)
        ]
        for copy in copies:
            copy.start()
        stores = []

        def store(src, dst):
            copy = pltpu.make_async_copy(src, dst, out_sems.at[len(stores)])
            copy.start()
            stores.append(copy)

        core = own_core()
        kept = pl.ds(pl.multiple_of(core * half, half), half)
        sent = pl.ds(pl.multiple_of((1 - core) * half, half), half)
        rate_columns = r_ref[...].T
        copies[0].wait()
        copies[1].wait()
        for row in range(0, tokens, ROWS):
            rows = slice(row, row + ROWS)
            k = k_ref[rows, :]
            h1 = dot(k, w_ref[0])
            if row == 0:
                copies[2].wait()
            h3 = dot(k, w_ref[1])
            sig = sigmoid(h1)
            act = h1 * sig
            hidden[rows, :] = (act * h3).astype(bf16)
            store(hidden.at[rows, :], factors_out.at[rows, width : 2 * width])
            if row == 0:
                copies[3].wait()
            for part in range(row, row + ROWS, lanes):
                rate = rate_columns[:, part // lanes : part // lanes + 1]
                span = slice(part, part + lanes)
                errors[span, :] = (-rate * v_ref[span, :].astype(f32)).astype(bf16)
            store(errors.at[rows, kept], factors_out.at[rows, 2 * width :])
            if row == 0:
                copies[4].wait()
            dz = dot_nt(errors[rows, :], w_ref[2])
            slope = sig + act * (1.0 - sig)
            grads[core, rows, :] = (dz * h3 * slope).astype(bf16)
            grads[1 - core, rows, :] = (dz * act).astype(bf16)
            store(grads.at[0, rows, :], factors_out.at[rows, :width])
        shared_send[...] = dot_tn(hidden[...], errors[:, sent]).astype(bf16)
        store(shared_send, shared_out)
        for row in range(0, width, ROWS):
            rows = slice(row, row + ROWS)
            own_send[rows, :] = dot_tn(k_ref[:, rows], grads[1]).astype(bf16)
            store(own_send.at[rows, :], own_out.at[rows, :])
        for copy in stores:
            copy.wait()

    results = [(width, width), (width, half), (tokens, 2 * width + half)]
    wide = pltpu.VMEM((tokens, width), bf16)
    return call(
        body,
        [shape(*dims) for dims in results],
        [VMEM] + [HBM] * 3,
        [wide, wide, pltpu.VMEM((3, width, width), bf16), wide, wide]
        + [pltpu.VMEM((2, tokens, width), bf16)]
        + [pltpu.VMEM(dims, bf16) for dims in results[:2]]
        + [pltpu.SemaphoreType.DMA((5,)), pltpu.SemaphoreType.DMA((3 * parts + 1 + width // ROWS,))],
        60,
        9 * tokens * width * width,
        12 * width * width,
        "gradients",
        [HBM] * len(results),
    )(rates, keys, values, weights)


def keep(keys, factors):
    width = keys.shape[1]
    half = width // 2

    def body(k_ref, f_ref, own, shared):
        own[...] = dot_tn(k_ref[...], f_ref[:, :width])
        shared[...] = dot_tn(f_ref[:, width : 2 * width], f_ref[:, 2 * width :])

    return call(
        body,
        [shape(width, width, dtype=f32), shape(width, half, dtype=f32)],
        [VMEM] * 2,
        [],
        16,
        3 * keys.shape[0] * width * width,
        9 * width * width,
        "keep",
    )(keys, factors)


def chip_sum(own_keep, own_got, shared_keep, shared_got):
    width, half = shared_keep.shape
    cut = width // NY // 2
    wide = width + half

    def body(ok_ref, og_ref, sk_ref, sg_ref, *outs):
        for n, out in enumerate(outs):
            block = lax.rem(own_y() + n // 2, NY) * 2
            side = own_parity() if n % 2 == 0 else 1 - own_parity()
            span = pl.ds(pl.multiple_of((block + side) * cut, cut), cut)
            own = ok_ref[span, :] + og_ref[span, :].astype(f32)
            shared = sk_ref[span, :] + sg_ref[span, :].astype(f32)
            out[:, :width] = own.astype(out.dtype)
            out[:, width:] = shared.astype(out.dtype)

    return call(
        body,
        [shape(cut, wide, dtype=f32)] + [shape(cut, wide)] * (2 * NY - 1),
        [VMEM] * 4,
        [],
        16,
        0,
        10 * width * wide,
        "chip_sum",
    )(own_keep, own_got, shared_keep, shared_got)


def assemble(own, previous, following, opposite):
    rows, wide = own.shape
    width = rows * NY
    pieces = [own, *following, *opposite, *previous]

    def body(own_ref, *rest):
        parts, (x_ref, s_ref) = rest[:-2], rest[-2:]
        base = own_y()
        start = pl.multiple_of(base * rows, rows)
        x_ref[pl.ds(start, rows), :] = own_ref[:, :width]
        s_ref[pl.ds(start, rows), :] = own_ref[:, width:]
        for n, part in enumerate(parts):
            cut = rows // 2
            start = lax.rem(base + 1 + n // 2, NY) * rows + (n % 2) * cut
            span = pl.ds(pl.multiple_of(start, cut), cut)
            x_ref[span, :] = part[:, :width]
            s_ref[span, :] = part[:, width:]

    return call(
        body,
        [shape(width, width), shape(width, wide - width)],
        [VMEM] * len(pieces),
        [],
        16,
        0,
        4 * width * wide,
        "assemble",
    )(*pieces)


def newton_schulz(x_ref, w_ref, outs, gram, poly, other):
    width = x_ref.shape[0]
    blocks = [slice(row, row + ROWS) for row in range(0, width, ROWS)]

    def store(ref, n, below):
        rows = blocks[n]
        ref[rows, : rows.stop] = below
        for column in blocks[:n]:
            ref[column, rows] = below[:, column].T

    square_sum = jnp.zeros((1, 1), f32)
    for rows in blocks:
        wide = x_ref[rows, :].astype(f32)
        square_sum = square_sum + jnp.sum(wide * wide).reshape(1, 1)
    scale = 1.0 / (jnp.sqrt(square_sum) + eps)
    now = x_ref
    for turn in range(NS_ITERS):
        for n, rows in enumerate(blocks):
            product = dot_nt(now[rows, :], now[: rows.stop, :])
            if turn == 0:
                product = product * (scale * scale)
            store(gram, n, product.astype(bf16))
        for n, rows in enumerate(blocks):
            squared = dot(gram[rows, :], gram[:, : rows.stop])
            linear = gram[rows, : rows.stop].astype(f32)
            store(poly, n, (ns_b * linear + ns_c * squared).astype(bf16))
        for rows in blocks:
            new = ns_a * now[rows, :].astype(f32) + dot(poly[rows, :], now[...])
            if turn == 0:
                new = new * scale
            new = new.astype(bf16)
            if turn < NS_ITERS - 1:
                other[rows, :] = new
            else:
                step = step_scale * new.astype(f32)
                fresh = (w_ref[rows, :].astype(f32) - step).astype(bf16)
                for n, out in enumerate(outs):
                    height = out.shape[0]
                    start, stop = max(rows.start, n * height), min(rows.stop, (n + 1) * height)
                    if start < stop:
                        inside = slice(start - n * height, stop - n * height)
                        out[inside, :] = fresh[start - rows.start : stop - rows.start]
        now = other


def own_step(summed, weights):
    width = weights.shape[-1]

    def body(x_ref, w_ref, top, bottom, gram, poly, other):
        newton_schulz(x_ref, w_ref.at[0, own_core()], (top, bottom), gram, poly, other)

    return call(
        body,
        [shape(width // 2, width)] * 2,
        [VMEM] * 2,
        [pltpu.VMEM((width, width), bf16)] * 3,
        16,
        10 * width**3,
        6 * width * width,
        "own_step",
    )(summed, weights)


def shared_step(mine, partners, weights):
    width = weights.shape[-1]
    half = width // 2

    def body(a_ref, b_ref, w_ref, out_ref, gram, poly, other, x_ref):
        first = own_core() == 0
        x_ref[:, :half] = jnp.where(first, a_ref[...], b_ref[...])
        x_ref[:, half:] = jnp.where(first, b_ref[...], a_ref[...])
        newton_schulz(x_ref, w_ref.at[0, 2], (out_ref,), gram, poly, other)

    return call(
        body,
        shape(width, width),
        [VMEM] * 3,
        [pltpu.VMEM((width, width), bf16)] * 4,
        16,
        10 * width**3,
        6 * width * width,
        "shared_step",
    )(mine, partners, weights)


def project(queries, own, other, shared, out_proj):
    tokens, width = queries.shape
    heads = out_proj.shape[1] // width

    half = width // 2

    def body(q_ref, own_a, own_b, other_a, other_b, shared_ref, p_ref, *outs):
        first = own_core() == 0
        left, right = q_ref[:, :half], q_ref[:, half:]
        q_own = dot(left, own_a[...]) + dot(right, own_b[...])
        q_other = dot(left, other_a[...]) + dot(right, other_b[...])
        q1 = jnp.where(first, q_own, q_other)
        q3 = jnp.where(first, q_other, q_own)
        gated = (q1 * sigmoid(q1) * q3).astype(bf16)
        outputs = dot(gated, shared_ref[...]).astype(bf16)
        cut = tokens // 2
        for step in range(heads):
            head = lax.rem(lax.axis_index("head") + step, heads)
            start = pl.multiple_of(head * width, width)
            product = dot(outputs, p_ref[:, pl.ds(start, width)])
            if step == 0:
                outs[0][...] = product
            else:
                outs[2 * step - 1][...] = product[:cut].astype(bf16)
                outs[2 * step][...] = product[cut:].astype(bf16)

    return call(
        body,
        [shape(tokens, width, dtype=f32)] + [shape(tokens // 2, width)] * (2 * heads - 2),
        [VMEM] * 7,
        [],
        20,
        2 * tokens * width * width * (3 + heads),
        16 * width * width,
        "project",
    )(queries, *own, *other, shared, out_proj)


def mix(own, sum_a, sum_b, direct_a, direct_b):
    tokens, width = own.shape
    cut = tokens // 2

    def body(sum_a_ref, sum_b_ref, direct_a_ref, direct_b_ref, own_ref, out):
        halves = [(sum_a_ref, direct_a_ref), (sum_b_ref, direct_b_ref)]
        for part, (relayed, direct) in enumerate(halves):
            span = slice(part * cut, (part + 1) * cut)
            total = own_ref[span, :] + relayed[...].astype(f32) + direct[...].astype(f32)
            out[:, span] = total.T.astype(bf16)

    return call(
        body, shape(width, tokens), [VMEM] * 5, [], 16, 0, 12 * tokens * width, "mix"
    )(sum_a, sum_b, direct_a, direct_b, own)


def shift(array, axis, pairs):
    return lax.ppermute(array, axis, pairs)


def add(left, right):
    return (left.astype(f32) + right.astype(f32)).astype(bf16)


def ring_sum(pieces, axis, up, down):
    next_a, next_b, far_a, far_b, previous_a, previous_b = pieces
    relay_a = shift(far_a, axis, up)
    relay_b = shift(far_b, axis, down)
    from_down_b = shift(next_b, axis, up)
    from_up_a = shift(previous_a, axis, down)
    from_down_a = shift(add(next_a, relay_a), axis, up)
    from_up_b = shift(add(previous_b, relay_b), axis, down)
    return from_down_a, from_up_b, from_up_a, from_down_b


def y_parity_sum(mine, mine_z, next_x, next_z, far_x, far_z, previous_x, previous_z):
    relay_x = shift(far_x, "tok", moved(1, 0))
    relay_z = shift(far_z, "tok", moved(-1, 0))
    sum_x = shift(add(next_x, relay_x), "tok", moved(1, 0))
    sum_z = shift(add(previous_z, relay_z), "tok", moved(-1, 1))
    direct_x = shift(previous_x, "tok", moved(-1, 0))
    beside = shift(mine_z, "tok", moved(0, 1))
    direct_z = shift(next_z, "tok", moved(1, 1))
    total = sum_x.astype(f32) + sum_z.astype(f32)
    total = total + direct_x.astype(f32) + beside.astype(f32)
    return (total + direct_z.astype(f32) + mine).astype(bf16)


def sum_and_spread(blocks, times):
    def body(in_ref, out_ref):
        total = in_ref[0].astype(f32)
        for n in range(1, blocks.shape[0]):
            total = total + in_ref[n].astype(f32)
        for n in range(times):
            out_ref[n] = total.astype(bf16)

    spread = shape(times, *blocks.shape[1:])
    return call(body, spread, [VMEM], [], 16, 0, 6 * blocks.size, "sum_and_spread")(blocks)


def ring_gather(block, axis, up, down):
    cut = block.shape[0] // 2
    block_a, block_b = block[:cut], block[cut:]
    previous_a = shift(block_a, axis, up)
    following_b = shift(block_b, axis, down)
    previous_b = shift(block_b, axis, up)
    following_a = shift(block_a, axis, down)
    far_a = shift(previous_a, axis, up)
    far_b = shift(following_b, axis, down)
    return (previous_a, previous_b), (following_a, following_b), (far_a, far_b)


def on_device(keys, values, rates, fast_weights, queries, out_proj):
    width = fast_weights.shape[-1]
    heads = lax.axis_size("head")

    own_send, shared_send, factors = gradients(
        keys, values, rates.reshape(-1, 128), fast_weights
    )
    own_got = swap_cores(own_send)
    shared_got = swap_cores(shared_send)
    own_keep, shared_keep = keep(keys, factors)
    shares = chip_sum(own_keep, own_got, shared_keep, shared_got)

    y_sum = y_parity_sum(*shares)
    shares = exchange(y_sum.reshape(NZ // 2, width // NY // NZ, -1), PARITY_GROUPS)
    rows = exchange(sum_and_spread(shares, NZ), Z_GROUPS).reshape(width // NY, -1)
    previous, following, far = ring_gather(rows, "tok", moved(1, 0), moved(-1, 0))
    own_sum, shared_part = assemble(rows, previous, following, far)

    shared_other = swap_cores(shared_part)
    own_fresh = own_step(own_sum, fast_weights)
    other_fresh = [swap_cores(rows) for rows in own_fresh]
    shared_fresh = shared_step(shared_part, shared_other, fast_weights)

    mixed, *shares = project(queries, own_fresh, other_fresh, shared_fresh, out_proj)
    up = [(i, (i + 1) % heads) for i in range(heads)]
    down = [(i, (i - 1) % heads) for i in range(heads)]
    return mix(mixed, *ring_sum(shares, "head", up, down))


def solution(mesh):
    in_specs = (
        P("tok", "head"),
        P("tok", "head"),
        P("tok", "head"),
        P("head", None, None, None),
        P("tok", "head"),
        P("head", None),
    )
    out_specs = P("head", "tok")
    return jax.shard_map(
        on_device, mesh=mesh, in_specs=in_specs, out_specs=out_specs, check_vma=False
    )
```

```python
import jax
import jax.numpy as jnp
from jax import lax
from jax.experimental import pallas as pl
from jax.experimental.pallas import tpu as pltpu
from jax.sharding import PartitionSpec as P

NS_ITERS = 2


ns_a = 3.4445
ns_b = -4.775
ns_c = 2.0315
step_scale = 1.0
eps = 1e-07

f32 = jnp.float32
bf16 = jnp.bfloat16

NY, NZ, NC = 4, 8, 2
ROWS = 256


def chip_index(y, z, core):
    return (y * NZ + z) * NC + core


Z_GROUPS = [
    [chip_index(y, z, core) for parity in range(2) for z in reversed(range(parity, NZ, 2))]
    for y in range(NY)
    for core in range(NC)
]
PARITY_GROUPS = [
    [chip_index(y, z, core) for z in reversed(range(parity, NZ, 2))]
    for y in range(NY)
    for parity in range(2)
    for core in range(NC)
]


def moved(up, flip):
    return [
        (chip_index(y, z, core), chip_index((y + up) % NY, z ^ flip, core))
        for y in range(NY)
        for z in range(NZ)
        for core in range(NC)
    ]


CORE_SWAP = [(device, device ^ 1) for device in range(NY * NZ * NC)]

VMEM = pl.BlockSpec(memory_space=pltpu.VMEM)
HBM = pl.BlockSpec(memory_space=pltpu.HBM)


def swap_cores(array):
    return lax.ppermute(array, "tok", CORE_SWAP)


def exchange(blocks, groups):
    return lax.all_to_all(blocks, "tok", 0, 0, axis_index_groups=groups)


def dot(left, right):
    return jnp.dot(left, right, preferred_element_type=f32)


def dot_nt(left, right):
    return lax.dot_general(left, right, (((1,), (1,)), ((), ())), preferred_element_type=f32)


def dot_tn(left, right):
    return lax.dot_general(left, right, (((0,), (0,)), ((), ())), preferred_element_type=f32)


def sigmoid(x):
    return 0.5 + 0.5 * jnp.tanh(0.5 * x)


def call(body, outs, in_specs, scratch, mib, flops, moved, name, out_specs=None):
    if out_specs is None:
        out_specs = [VMEM] * len(outs) if isinstance(outs, list) else VMEM
    return pl.pallas_call(
        body,
        out_shape=outs,
        in_specs=in_specs,
        out_specs=out_specs,
        scratch_shapes=scratch,
        compiler_params=pltpu.CompilerParams(vmem_limit_bytes=mib << 20),
        cost_estimate=pl.CostEstimate(flops=flops, bytes_accessed=moved, transcendentals=0),
        name=name,
    )


def own_core():
    return lax.rem(lax.axis_index("tok"), NC)


def own_parity():
    return lax.rem(lax.div(lax.axis_index("tok"), NC), 2)


def own_y():
    return lax.div(lax.axis_index("tok"), NZ * NC)


def shape(*dims, dtype=bf16):
    return jax.ShapeDtypeStruct(dims, dtype)


def gradients(keys, values, rates, weights):
    tokens, width = keys.shape
    half = width // 2
    lanes = rates.shape[1]
    parts = tokens // ROWS

    def body(r_ref, k_hbm, v_hbm, w_hbm, own_out, shared_out, factors_out,
             k_ref, v_ref, w_ref, errors, hidden, grads, own_send, shared_send, sems, out_sems):
        moves = [
            (k_hbm, k_ref),
            (w_hbm.at[0, 0], w_ref.at[0]),
            (w_hbm.at[0, 1], w_ref.at[1]),
            (v_hbm, v_ref),
            (w_hbm.at[0, 2], w_ref.at[2]),
        ]
        copies = [
            pltpu.make_async_copy(src, dst, sems.at[n]) for n, (src, dst) in enumerate(moves)
        ]
        for copy in copies:
            copy.start()
        stores = []

        def store(src, dst):
            copy = pltpu.make_async_copy(src, dst, out_sems.at[len(stores)])
            copy.start()
            stores.append(copy)

        core = own_core()
        kept = pl.ds(pl.multiple_of(core * half, half), half)
        sent = pl.ds(pl.multiple_of((1 - core) * half, half), half)
        rate_columns = r_ref[...].T
        copies[0].wait()
        copies[1].wait()
        for row in range(0, tokens, ROWS):
            rows = slice(row, row + ROWS)
            k = k_ref[rows, :]
            h1 = dot(k, w_ref[0])
            if row == 0:
                copies[2].wait()
            h3 = dot(k, w_ref[1])
            sig = sigmoid(h1)
            act = h1 * sig
            hidden[rows, :] = (act * h3).astype(bf16)
            store(hidden.at[rows, :], factors_out.at[rows, width : 2 * width])
            if row == 0:
                copies[3].wait()
            for part in range(row, row + ROWS, lanes):
                rate = rate_columns[:, part // lanes : part // lanes + 1]
                span = slice(part, part + lanes)
                errors[span, :] = (-rate * v_ref[span, :].astype(f32)).astype(bf16)
            store(errors.at[rows, kept], factors_out.at[rows, 2 * width :])
            if row == 0:
                copies[4].wait()
            dz = dot_nt(errors[rows, :], w_ref[2])
            slope = sig + act * (1.0 - sig)
            grads[core, rows, :] = (dz * h3 * slope).astype(bf16)
            grads[1 - core, rows, :] = (dz * act).astype(bf16)
            store(grads.at[0, rows, :], factors_out.at[rows, :width])
        shared_send[...] = dot_tn(hidden[...], errors[:, sent]).astype(bf16)
        store(shared_send, shared_out)
        for row in range(0, width, ROWS):
            rows = slice(row, row + ROWS)
            own_send[rows, :] = dot_tn(k_ref[:, rows], grads[1]).astype(bf16)
            store(own_send.at[rows, :], own_out.at[rows, :])
        for copy in stores:
            copy.wait()

    results = [(width, width), (width, half), (tokens, 2 * width + half)]
    wide = pltpu.VMEM((tokens, width), bf16)
    return call(
        body,
        [shape(*dims) for dims in results],
        [VMEM] + [HBM] * 3,
        [wide, wide, pltpu.VMEM((3, width, width), bf16), wide, wide]
        + [pltpu.VMEM((2, tokens, width), bf16)]
        + [pltpu.VMEM(dims, bf16) for dims in results[:2]]
        + [pltpu.SemaphoreType.DMA((5,)), pltpu.SemaphoreType.DMA((3 * parts + 1 + width // ROWS,))],
        60,
        9 * tokens * width * width,
        12 * width * width,
        "gradients",
        [HBM] * len(results),
    )(rates, keys, values, weights)


def keep(keys, factors):
    width = keys.shape[1]
    half = width // 2

    def body(k_ref, f_ref, own, shared):
        own[...] = dot_tn(k_ref[...], f_ref[:, :width])
        shared[...] = dot_tn(f_ref[:, width : 2 * width], f_ref[:, 2 * width :])

    return call(
        body,
        [shape(width, width, dtype=f32), shape(width, half, dtype=f32)],
        [VMEM] * 2,
        [],
        16,
        3 * keys.shape[0] * width * width,
        9 * width * width,
        "keep",
    )(keys, factors)


def chip_sum(own_keep, own_got, shared_keep, shared_got):
    width, half = shared_keep.shape
    cut = width // NY // 2
    wide = width + half

    def body(ok_ref, og_ref, sk_ref, sg_ref, *outs):
        for n, out in enumerate(outs):
            block = lax.rem(own_y() + n // 2, NY) * 2
            side = own_parity() if n % 2 == 0 else 1 - own_parity()
            span = pl.ds(pl.multiple_of((block + side) * cut, cut), cut)
            own = ok_ref[span, :] + og_ref[span, :].astype(f32)
            shared = sk_ref[span, :] + sg_ref[span, :].astype(f32)
            out[:, :width] = own.astype(out.dtype)
            out[:, width:] = shared.astype(out.dtype)

    return call(
        body,
        [shape(cut, wide, dtype=f32)] + [shape(cut, wide)] * (2 * NY - 1),
        [VMEM] * 4,
        [],
        16,
        0,
        10 * width * wide,
        "chip_sum",
    )(own_keep, own_got, shared_keep, shared_got)


def assemble(own, previous, following, opposite):
    rows, wide = own.shape
    width = rows * NY
    pieces = [own, *following, *opposite, *previous]

    def body(own_ref, *rest):
        parts, (x_ref, s_ref) = rest[:-2], rest[-2:]
        base = own_y()
        start = pl.multiple_of(base * rows, rows)
        x_ref[pl.ds(start, rows), :] = own_ref[:, :width]
        s_ref[pl.ds(start, rows), :] = own_ref[:, width:]
        for n, part in enumerate(parts):
            cut = rows // 2
            start = lax.rem(base + 1 + n // 2, NY) * rows + (n % 2) * cut
            span = pl.ds(pl.multiple_of(start, cut), cut)
            x_ref[span, :] = part[:, :width]
            s_ref[span, :] = part[:, width:]

    return call(
        body,
        [shape(width, width), shape(width, wide - width)],
        [VMEM] * len(pieces),
        [],
        16,
        0,
        4 * width * wide,
        "assemble",
    )(*pieces)


def newton_schulz(x_ref, w_ref, outs, gram, poly, other):
    width = x_ref.shape[0]
    blocks = [slice(row, row + ROWS) for row in range(0, width, ROWS)]

    def store(ref, n, below):
        rows = blocks[n]
        ref[rows, : rows.stop] = below
        for column in blocks[:n]:
            ref[column, rows] = below[:, column].T

    square_sum = jnp.zeros((1, 1), f32)
    for rows in blocks:
        wide = x_ref[rows, :].astype(f32)
        square_sum = square_sum + jnp.sum(wide * wide).reshape(1, 1)
    scale = 1.0 / (jnp.sqrt(square_sum) + eps)
    now = x_ref
    for turn in range(NS_ITERS):
        for n, rows in enumerate(blocks):
            product = dot_nt(now[rows, :], now[: rows.stop, :])
            if turn == 0:
                product = product * (scale * scale)
            store(gram, n, product.astype(bf16))
        for n, rows in enumerate(blocks):
            squared = dot(gram[rows, :], gram[:, : rows.stop])
            linear = gram[rows, : rows.stop].astype(f32)
            store(poly, n, (ns_b * linear + ns_c * squared).astype(bf16))
        for rows in blocks:
            new = ns_a * now[rows, :].astype(f32) + dot(poly[rows, :], now[...])
            if turn == 0:
                new = new * scale
            new = new.astype(bf16)
            if turn < NS_ITERS - 1:
                other[rows, :] = new
            else:
                step = step_scale * new.astype(f32)
                fresh = (w_ref[rows, :].astype(f32) - step).astype(bf16)
                for n, out in enumerate(outs):
                    height = out.shape[0]
                    start, stop = max(rows.start, n * height), min(rows.stop, (n + 1) * height)
                    if start < stop:
                        inside = slice(start - n * height, stop - n * height)
                        out[inside, :] = fresh[start - rows.start : stop - rows.start]
        now = other


def own_step(summed, weights):
    width = weights.shape[-1]

    def body(x_ref, w_ref, top, bottom, gram, poly, other):
        newton_schulz(x_ref, w_ref.at[0, own_core()], (top, bottom), gram, poly, other)

    return call(
        body,
        [shape(width // 2, width)] * 2,
        [VMEM] * 2,
        [pltpu.VMEM((width, width), bf16)] * 3,
        16,
        10 * width**3,
        6 * width * width,
        "own_step",
    )(summed, weights)


def shared_step(mine, partners, weights):
    width = weights.shape[-1]
    half = width // 2

    def body(a_ref, b_ref, w_ref, out_ref, gram, poly, other, x_ref):
        first = own_core() == 0
        x_ref[:, :half] = jnp.where(first, a_ref[...], b_ref[...])
        x_ref[:, half:] = jnp.where(first, b_ref[...], a_ref[...])
        newton_schulz(x_ref, w_ref.at[0, 2], (out_ref,), gram, poly, other)

    return call(
        body,
        shape(width, width),
        [VMEM] * 3,
        [pltpu.VMEM((width, width), bf16)] * 4,
        16,
        10 * width**3,
        6 * width * width,
        "shared_step",
    )(mine, partners, weights)


def projected(outputs, p_ref, step, heads):
    width = p_ref.shape[0]
    head = lax.rem(lax.axis_index("head") + step, heads)
    start = pl.multiple_of(head * width, width)
    return dot(outputs, p_ref[:, pl.ds(start, width)])


def target_outputs(queries, own, other, shared, out_proj):
    tokens, width = queries.shape
    heads = out_proj.shape[1] // width
    half = width // 2
    cut = tokens // 2

    def body(q_ref, own_a, own_b, other_a, other_b, shared_ref, p_ref, out, far_a, far_b):
        first = own_core() == 0
        left, right = q_ref[:, :half], q_ref[:, half:]
        q_own = dot(left, own_a[...]) + dot(right, own_b[...])
        q_other = dot(left, other_a[...]) + dot(right, other_b[...])
        q1 = jnp.where(first, q_own, q_other)
        q3 = jnp.where(first, q_other, q_own)
        gated = (q1 * sigmoid(q1) * q3).astype(bf16)
        outputs = dot(gated, shared_ref[...]).astype(bf16)
        out[...] = outputs
        product = projected(outputs, p_ref, 2, heads).astype(bf16)
        far_a[...] = product[:cut]
        far_b[...] = product[cut:]

    return call(
        body,
        [shape(tokens, width), shape(cut, width), shape(cut, width)],
        [VMEM] * 7,
        [],
        20,
        8 * tokens * width * width,
        16 * width * width,
        "target_outputs",
    )(queries, *own, *other, shared, out_proj)


def project_near(outputs, out_proj):
    tokens, width = outputs.shape
    heads = out_proj.shape[1] // width
    cut = tokens // 2

    def body(o_ref, p_ref, mine, next_a, next_b, previous_a, previous_b):
        for step, top, bottom in ((1, next_a, next_b), (3, previous_a, previous_b)):
            product = projected(o_ref[...], p_ref, step, heads).astype(bf16)
            top[...] = product[:cut]
            bottom[...] = product[cut:]
        mine[...] = projected(o_ref[...], p_ref, 0, heads)

    return call(
        body,
        [shape(tokens, width, dtype=f32)] + [shape(cut, width)] * 4,
        [VMEM] * 2,
        [],
        16,
        6 * tokens * width * width,
        8 * width * width,
        "project_near",
    )(outputs, out_proj)


def mix(own, sum_a, sum_b, direct_a, direct_b):
    tokens, width = own.shape
    cut = tokens // 2

    def body(sum_a_ref, sum_b_ref, direct_a_ref, direct_b_ref, own_ref, out):
        halves = [(sum_a_ref, direct_a_ref), (sum_b_ref, direct_b_ref)]
        for part, (relayed, direct) in enumerate(halves):
            span = slice(part * cut, (part + 1) * cut)
            total = own_ref[span, :] + relayed[...].astype(f32) + direct[...].astype(f32)
            out[:, span] = total.T.astype(bf16)

    return call(
        body, shape(width, tokens), [VMEM] * 5, [], 16, 0, 12 * tokens * width, "mix"
    )(sum_a, sum_b, direct_a, direct_b, own)


def shift(array, axis, pairs):
    return lax.ppermute(array, axis, pairs)


def add(left, right):
    return (left.astype(f32) + right.astype(f32)).astype(bf16)


def ring_sum(pieces, axis, up, down):
    next_a, next_b, far_a, far_b, previous_a, previous_b = pieces
    relay_a = shift(far_a, axis, up)
    relay_b = shift(far_b, axis, down)
    from_down_b = shift(next_b, axis, up)
    from_up_a = shift(previous_a, axis, down)
    from_down_a = shift(add(next_a, relay_a), axis, up)
    from_up_b = shift(add(previous_b, relay_b), axis, down)
    return from_down_a, from_up_b, from_up_a, from_down_b


def y_parity_sum(mine, mine_z, next_x, next_z, far_x, far_z, previous_x, previous_z):
    relay_x = shift(far_x, "tok", moved(1, 0))
    relay_z = shift(far_z, "tok", moved(-1, 0))
    sum_x = shift(add(next_x, relay_x), "tok", moved(1, 0))
    sum_z = shift(add(previous_z, relay_z), "tok", moved(-1, 1))
    direct_x = shift(previous_x, "tok", moved(-1, 0))
    beside = shift(mine_z, "tok", moved(0, 1))
    direct_z = shift(next_z, "tok", moved(1, 1))
    total = sum_x.astype(f32) + sum_z.astype(f32)
    total = total + direct_x.astype(f32) + beside.astype(f32)
    return (total + direct_z.astype(f32) + mine).astype(bf16)


def sum_and_spread(blocks, times):
    def body(in_ref, out_ref):
        total = in_ref[0].astype(f32)
        for n in range(1, blocks.shape[0]):
            total = total + in_ref[n].astype(f32)
        for n in range(times):
            out_ref[n] = total.astype(bf16)

    spread = shape(times, *blocks.shape[1:])
    return call(body, spread, [VMEM], [], 16, 0, 6 * blocks.size, "sum_and_spread")(blocks)


def ring_gather(block, axis, up, down):
    cut = block.shape[0] // 2
    block_a, block_b = block[:cut], block[cut:]
    previous_a = shift(block_a, axis, up)
    following_b = shift(block_b, axis, down)
    previous_b = shift(block_b, axis, up)
    following_a = shift(block_a, axis, down)
    far_a = shift(previous_a, axis, up)
    far_b = shift(following_b, axis, down)
    return (previous_a, previous_b), (following_a, following_b), (far_a, far_b)


def on_device(keys, values, rates, fast_weights, queries, out_proj):
    width = fast_weights.shape[-1]
    heads = lax.axis_size("head")

    own_send, shared_send, factors = gradients(
        keys, values, rates.reshape(-1, 128), fast_weights
    )
    own_got = swap_cores(own_send)
    shared_got = swap_cores(shared_send)
    own_keep, shared_keep = keep(keys, factors)
    shares = chip_sum(own_keep, own_got, shared_keep, shared_got)

    y_sum = y_parity_sum(*shares)
    shares = exchange(y_sum.reshape(NZ // 2, width // NY // NZ, -1), PARITY_GROUPS)
    rows = exchange(sum_and_spread(shares, NZ), Z_GROUPS).reshape(width // NY, -1)
    previous, following, far = ring_gather(rows, "tok", moved(1, 0), moved(-1, 0))
    own_sum, shared_part = assemble(rows, previous, following, far)

    shared_other = swap_cores(shared_part)
    own_fresh = own_step(own_sum, fast_weights)
    other_fresh = [swap_cores(rows) for rows in own_fresh]
    shared_fresh = shared_step(shared_part, shared_other, fast_weights)

    outputs, far_a, far_b = target_outputs(
        queries, own_fresh, other_fresh, shared_fresh, out_proj
    )
    mixed, next_a, next_b, previous_a, previous_b = project_near(outputs, out_proj)
    shares = [next_a, next_b, far_a, far_b, previous_a, previous_b]
    up = [(i, (i + 1) % heads) for i in range(heads)]
    down = [(i, (i - 1) % heads) for i in range(heads)]
    return mix(mixed, *ring_sum(shares, "head", up, down))


def solution(mesh):
    in_specs = (
        P("tok", "head"),
        P("tok", "head"),
        P("tok", "head"),
        P("head", None, None, None),
        P("tok", "head"),
        P("head", None),
    )
    out_specs = P("head", "tok")
    return jax.shard_map(
        on_device, mesh=mesh, in_specs=in_specs, out_specs=out_specs, check_vma=False
    )
```
